512 devices in a mesh: pool: 64 (over y_lo, z, core), tensor: 8 (over y_hi, x).
Axes of the slice: x: 4, y: 8 (y_hi: 2, y_lo: 4; y = y_hi * 4 + y_lo), z: 8, core: 2. Of those that a mesh axis runs over, the one named last changes fastest.
Arguments:
- queries: bfloat16 [2, 1024, 8192], P(None, 'pool', 'tensor'), may hold values from -160 to 160
- new_keys: bfloat16 [2, 1024, 1024], P(None, 'pool', 'tensor'), may hold values from -10 to 10
- new_values: bfloat16 [2, 1024, 1024], P(None, 'pool', 'tensor'), may hold values from -6 to 6
- cache_keys: bfloat16 [1024, 128, 1024], P('pool', None, 'tensor'), may hold values from -5 to 5
- cache_values: bfloat16 [1024, 128, 1024], P('pool', None, 'tensor'), may hold values from -6 to 6
- cache_lengths: int32 [1024], P('pool'), may hold values from 2 to 128
- handoff_kv: bfloat16 [64, 48, 8, 2, 1024], P('pool', None, 'tensor'), may hold values from -6 to 6
- page_owner: int32 [3072], replicated, may hold values from 0 to 63, as said below
- page_request: int32 [3072], replicated, may hold values from 0 to 1
- page_length: int32 [3072], replicated, may hold values from 1 to 8
Outputs:
- attended: bfloat16 [2, 1024, 8192], P(None, 'pool', 'tensor')
The draws below stay inside these ranges and needn't reach their ends.
Inputs may be any that keep to these rules, and one draw needn't show every extreme that they name: `page_owner`: no source instance hands more than 2 pages to one decode instance.
All inputs are finite; a program needn't handle non-finite values.
Results may differ from the reference program's by a relative error of at most 0.0021.
Values may be sent and summed in bfloat16 or wider, within the bound.
No kernel may reach another device: no remote copies, remote signals or barrier semaphores. Data moves between devices by JAX's collectives and lax.ppermute only.
A program may use at most 64 MiB of HBM per device.

```python
import jax
import jax.numpy as jnp
from jax import lax

HEADS = 64
KV_HEADS = 8
HEAD_DIM = 128
SAMPLES = 8
REQ_DEV = 2
RES_LEN = 128
PAGE = 8
PAGES_DEV = 48
ROWS = 16
ALL_ROWS = 1024
CAP = 2
N_POOL = 64


def query_base(key):
    inner_key = jax.random.fold_in(key, 101)
    return 2.0 * jax.random.truncated_normal(inner_key, -3.0, 3.0, (2, ALL_ROWS, HEADS * HEAD_DIM), jnp.float32)


def key_base(key):
    inner_key = jax.random.fold_in(key, 202)
    return jax.random.truncated_normal(inner_key, -5.0, 5.0, (ALL_ROWS, RES_LEN, KV_HEADS * HEAD_DIM), jnp.float32)


def draw_queries(key, part):
    base_draw = query_base(key)
    return base_draw.astype(jnp.bfloat16)


def draw_cache_keys(key, part):
    base_draw = key_base(key)
    return base_draw.astype(jnp.bfloat16)


def draw_new_keys(key, part):
    base_draw = query_base(key)
    key = jax.random.fold_in(key, 7)
    group = HEADS // KV_HEADS
    shared_part = jnp.mean(base_draw.reshape(2, ALL_ROWS, KV_HEADS, group, HEAD_DIM), axis=3)
    noise_part = jax.random.truncated_normal(key, -4.0, 4.0, shared_part.shape, jnp.float32)
    return (shared_part + noise_part).reshape(2, ALL_ROWS, KV_HEADS * HEAD_DIM).astype(jnp.bfloat16)


def draw_page_owner(key, part):
    key = jax.random.fold_in(key, 9)
    hot_key, source_key = jax.random.split(key)
    hot_owner = jax.random.randint(hot_key, (), 0, N_POOL).astype(jnp.int32)

    def one_source(own_key):
        spot_key, order_key = jax.random.split(own_key)
        spot_ids = jax.random.permutation(spot_key, (N_POOL - 1) * CAP)[:PAGES_DEV - CAP].astype(jnp.int32)
        other_owner = spot_ids // CAP
        other_owner = other_owner + (other_owner >= hot_owner).astype(jnp.int32)
        owner_list = jnp.concatenate([jnp.full((CAP,), hot_owner, jnp.int32), other_owner])
        return owner_list[jax.random.permutation(order_key, PAGES_DEV)]
    owners_all = jax.vmap(one_source)(jax.random.split(source_key, N_POOL))
    return owners_all.reshape(N_POOL * PAGES_DEV).astype(jnp.int32)


def place_ends(result, stream_key, low, largest):
    index_at = [jax.random.randint(jax.random.fold_in(stream_key, axis), (), 0, length) for axis, length in enumerate(result.shape)]
    widest = result.shape.index(max(result.shape))
    neighbour = index_at[:widest] + [(index_at[widest] + 1) % result.shape[widest]] + index_at[widest + 1:]
    return result.at[tuple(index_at)].set(low).at[tuple(neighbour)].set(largest)


def block_scale(key, extent, shards, least, largest):
    def one(axis_at, parts):
        heights = jax.random.uniform(jax.random.fold_in(jax.random.fold_in(key, 6), axis_at), (parts,), jnp.float32, least / len(shards), largest / len(shards))
        return jnp.repeat(jnp.exp(heights), extent[axis_at] // parts).reshape((-1,) + (1,) * (len(extent) - axis_at - 1))

    loudness = one(*shards[0])
    for cut in shards[1:]:
        loudness = loudness * one(*cut)
    return loudness


def noise(key, dims, scale, limit, cuts=(), held_as=jnp.bfloat16):
    loudness = block_scale(key, dims, cuts, -0.22, 0.18) if cuts else 1.0
    result = jax.random.normal(key, dims, jnp.float32) * scale * loudness
    return jnp.minimum(jnp.maximum(result, -limit), limit).astype(held_as)


def setup_inputs(seed: int = 0) -> dict:
    seeds = jax.random.split(jax.random.key(seed), 11)
    return {
        "queries": draw_queries(jax.random.fold_in(seeds[10], 71), 0),
        "new_keys": draw_new_keys(jax.random.fold_in(seeds[10], 71), 0),
        "new_values": noise(seeds[2], (2, ALL_ROWS, KV_HEADS * HEAD_DIM), 1.0, 6.0, ((1, 64), (2, 8))),
        "cache_keys": draw_cache_keys(jax.random.fold_in(seeds[10], 71), 0),
        "cache_values": noise(seeds[4], (ALL_ROWS, RES_LEN, KV_HEADS * HEAD_DIM), 1.0, 6.0, ((0, 64), (2, 8))),
        "cache_lengths": place_ends(jax.random.randint(seeds[5], (ALL_ROWS,), 2, RES_LEN + 1), jax.random.fold_in(seeds[5], 1), 2, RES_LEN).astype(jnp.int32),
        "handoff_kv": noise(seeds[6], (N_POOL, PAGES_DEV, PAGE, 2, KV_HEADS * HEAD_DIM), 1.0, 6.0, ((0, 64), (2, 8))),
        "page_owner": draw_page_owner(jax.random.fold_in(seeds[10], 71), 0),
        "page_request": place_ends(jax.random.randint(seeds[8], (N_POOL * PAGES_DEV,), 0, REQ_DEV), jax.random.fold_in(seeds[8], 1), 0, REQ_DEV - 1).astype(jnp.int32),
        "page_length": place_ends(jax.random.randint(seeds[9], (N_POOL * PAGES_DEV,), 1, PAGE + 1), jax.random.fold_in(seeds[9], 1), 1, PAGE).astype(jnp.int32),
    }


MASKED_SCORE = -1.0e30


def page_slots(owner_table):
    page_count = owner_table.shape[1]
    same_owner = owner_table[:, :, None] == owner_table[:, None, :]
    position = jnp.arange(page_count, dtype=jnp.int32)
    before = position[None, :] < position[:, None]
    return jnp.sum(jnp.where(same_owner & before[None], 1, 0), axis=2).astype(jnp.int32)


def to_wide(values):
    return lax.optimization_barrier(values.astype(jnp.bfloat16)).astype(jnp.float32)


def reference(queries, new_keys, new_values, cache_keys, cache_values, cache_lengths, handoff_kv, page_owner, page_request, page_length):
    group = HEADS // KV_HEADS
    score_scale = HEAD_DIM ** -0.5
    owner_table = page_owner.reshape(N_POOL, PAGES_DEV)
    slot_table = page_slots(owner_table)
    request_table = page_request.reshape(N_POOL, PAGES_DEV)
    length_table = page_length.reshape(N_POOL, PAGES_DEV)
    page_ids = jnp.arange(PAGES_DEV, dtype=jnp.int32)
    slot_ids = jnp.arange(CAP, dtype=jnp.int32)
    source_ids = jnp.arange(N_POOL, dtype=jnp.int32)
    token_ids = jnp.arange(PAGE, dtype=jnp.int32)
    row_request = jnp.arange(ROWS, dtype=jnp.int32) // SAMPLES
    step_ids = jnp.arange(2, dtype=jnp.int32)
    fresh_mask = step_ids[None, :] <= step_ids[:, None]
    key_total = N_POOL * CAP * PAGE

    query_all = queries.reshape(2, N_POOL, ROWS, KV_HEADS, group, HEAD_DIM).transpose(1, 0, 2, 3, 4, 5)
    fresh_keys_all = new_keys.reshape(2, N_POOL, ROWS, KV_HEADS, HEAD_DIM).transpose(1, 0, 2, 3, 4)
    fresh_values_all = new_values.reshape(2, N_POOL, ROWS, KV_HEADS, HEAD_DIM).transpose(1, 0, 2, 3, 4)
    res_keys_all = cache_keys.reshape(N_POOL, ROWS, RES_LEN, KV_HEADS, HEAD_DIM)
    res_values_all = cache_values.reshape(N_POOL, ROWS, RES_LEN, KV_HEADS, HEAD_DIM)
    res_lengths_all = cache_lengths.reshape(N_POOL, ROWS)

    def instance(inputs):
        own_index, query_block, fresh_keys, fresh_values, res_keys, res_values, res_lengths = inputs
        matched = (owner_table[:, None, :] == own_index) & (slot_table[:, None, :] == slot_ids[None, :, None])
        page_index = jnp.sum(jnp.where(matched, page_ids[None, None, :], 0), axis=2).astype(jnp.int32)
        slot_request = jnp.sum(jnp.where(matched, request_table[:, None, :], 0), axis=2)
        slot_length = jnp.sum(jnp.where(matched, length_table[:, None, :], 0), axis=2)
        arrived = handoff_kv[source_ids[:, None], page_index]
        recv_keys = arrived[:, :, :, 0, :].reshape(key_total, KV_HEADS, HEAD_DIM).astype(jnp.float32)
        recv_values = arrived[:, :, :, 1, :].reshape(key_total, KV_HEADS, HEAD_DIM).astype(jnp.float32)
        live_token = (token_ids[None, None, :] < slot_length[:, :, None]).reshape(key_total)
        token_request = jnp.broadcast_to(slot_request[:, :, None], (N_POOL, CAP, PAGE)).reshape(key_total)
        recv_mask = (row_request[:, None] == token_request[None, :]) & live_token[None, :]
        res_mask = jnp.arange(RES_LEN, dtype=jnp.int32)[None, :] < res_lengths[:, None]
        query_wide = query_block.astype(jnp.float32)
        res_score = jnp.einsum("srkgd,rtkd->srkgt", query_wide, res_keys.astype(jnp.float32)) * score_scale
        res_score = jnp.where(res_mask[None, :, None, None, :], res_score, MASKED_SCORE)
        recv_score = jnp.einsum("srkgd,nkd->srkgn", query_wide, recv_keys) * score_scale
        recv_score = jnp.where(recv_mask[None, :, None, None, :], recv_score, MASKED_SCORE)
        fresh_score = jnp.einsum("srkgd,urkd->srkgu", query_wide, fresh_keys.astype(jnp.float32)) * score_scale
        fresh_score = jnp.where(fresh_mask[:, None, None, None, :], fresh_score, MASKED_SCORE)
        peak_score = jnp.maximum(jnp.maximum(jnp.max(res_score, axis=-1), jnp.max(recv_score, axis=-1)), jnp.max(fresh_score, axis=-1))[..., None]
        res_weight = jnp.exp(res_score - peak_score)
        recv_weight = jnp.exp(recv_score - peak_score)
        fresh_weight = jnp.exp(fresh_score - peak_score)
        denominator = jnp.sum(res_weight, axis=-1) + jnp.sum(recv_weight, axis=-1) + jnp.sum(fresh_weight, axis=-1)
        weighted = jnp.einsum("srkgt,rtkd->srkgd", to_wide(res_weight), res_values.astype(jnp.float32))
        weighted = weighted + jnp.einsum("srkgn,nkd->srkgd", to_wide(recv_weight), recv_values)
        weighted = weighted + jnp.einsum("srkgu,urkd->srkgd", to_wide(fresh_weight), fresh_values.astype(jnp.float32))
        result_block = (weighted / denominator[..., None]).astype(jnp.bfloat16)
        return result_block.reshape(2, ROWS, HEADS * HEAD_DIM)

    outputs = lax.map(instance, (source_ids, query_all, fresh_keys_all, fresh_values_all, res_keys_all, res_values_all, res_lengths_all))
    return outputs.transpose(1, 0, 2, 3).reshape(2, ALL_ROWS, HEADS * HEAD_DIM)
```

```python
import jax
import jax.numpy as jnp
from jax import lax
from jax.experimental import pallas as pl
from jax.experimental.pallas import tpu as pltpu
from jax.sharding import PartitionSpec as P

HEADS = 64
KV_HEADS = 8
HEAD_DIM = 128
GROUP = HEADS // KV_HEADS
SAMPLES = 8
POOL = 64
TENSOR = 8
PAGES = 48
CAP = 2
ROWS = 16
RES_LEN = 128
SLOTS = POOL * CAP
QUERIES = 2 * ROWS * GROUP

MASKED_SCORE = -1e30
SCORE_SCALE = HEAD_DIM ** (-0.5) * 1.4426950408889634

VMEM = pl.BlockSpec(memory_space=pltpu.VMEM)
SMEM = pl.BlockSpec(memory_space=pltpu.SMEM)
PARAMS = pltpu.CompilerParams(vmem_limit_bytes=32 * 1024 * 1024)


def iota(shape, axis):
    return lax.broadcasted_iota(jnp.int32, shape, axis)


def pack_kernel(owner_ref, pages_ref, out_ref):
    start = lax.axis_index("pool") * PAGES
    row, lane = start // 128, lax.rem(start, 128)
    shift = lax.rem(128 - lane, 128)
    first = jnp.broadcast_to(owner_ref[pl.ds(row, 1), :], (8, 128))
    second = jnp.broadcast_to(owner_ref[pl.ds(jnp.minimum(row + 1, 23), 1), :], (8, 128))
    lanes = iota((8, 128), 1)
    owners = jnp.where(lanes < 128 - lane, pltpu.roll(first, shift, 1), pltpu.roll(second, shift, 1))
    across = jnp.broadcast_to(owners[0:1].astype(jnp.float32), (128, 128))
    down = across.T
    earlier = iota((128, 128), 0) < iota((128, 128), 1)
    rank = jnp.sum(jnp.where((across == down) & earlier, 1.0, 0.0), axis=0, keepdims=True)
    key = (owners * (2 * CAP)).astype(jnp.float32) + 2.0 * rank
    key = key.astype(jnp.int32)
    target = jnp.where(
        lanes < PAGES, key, jnp.where(lanes < 2 * PAGES, pltpu.roll(key, PAGES, 1) + 1, -1)
    )
    slots = jnp.where(iota((2 * SLOTS, 128), 0) == target[0:1], 1.0, 0.0).astype(jnp.bfloat16)
    new = iota((256, 256), 0)
    old = iota((256, 256), 1)
    wanted = (new & 15) * 16 + (new >> 5) * 2 + ((new >> 4) & 1)
    swap = jnp.where(old == wanted, 1.0, 0.0).astype(jnp.bfloat16)
    turned = [
        jnp.dot(swap, pages_ref[256 * i : 256 * (i + 1), :], preferred_element_type=jnp.float32).astype(
            jnp.bfloat16
        )
        for i in range(3)
    ]
    zeros = jnp.zeros((128 - 2 * PAGES, 128), jnp.bfloat16)
    for head in range(0, KV_HEADS, 2):
        block = jnp.concatenate(
            [
                jnp.concatenate(
                    [turned[i][32 * h + 16 * kv : 32 * h + 16 * kv + 16] for kv in range(2) for i in range(3)]
                    + [zeros],
                    axis=0,
                )
                for h in (head, head + 1)
            ],
            axis=1,
        )
        placed = jnp.dot(slots, block, preferred_element_type=jnp.float32).astype(jnp.bfloat16)
        out_ref[head * 256 : head * 256 + 256, :] = placed[:, 0:128]
        out_ref[head * 256 + 256 : head * 256 + 512, :] = placed[:, 128:256]


def pack(owners, pages):
    return pl.pallas_call(
        pack_kernel,
        out_shape=jax.ShapeDtypeStruct((KV_HEADS * SLOTS * 2, 128), jnp.bfloat16),
        in_specs=[VMEM, VMEM],
        out_specs=VMEM,
        compiler_params=PARAMS,
        name="pack",
    )(owners, pages)


def resident_kernel(len_ref, q_ref, ck_ref, cv_ref, nk_ref, nv_ref, qt_ref, m_ref, l_ref, acc_ref, turn_ref):
    for step in range(2):
        wide = q_ref[step].astype(jnp.float32)
        for g in range(GROUP):
            turn_ref[pl.ds(step * GROUP + g, ROWS, stride=2 * GROUP), :] = wide[:, 128 * g : 128 * g + 128]
    query = turn_ref[...].astype(jnp.bfloat16)
    qt_ref[...] = query
    dims = (((1,), (1,)), ((), ()))
    lanes = iota((16, 128), 1)
    parts = []
    for r in range(ROWS):
        score = lax.dot_general(
            query[16 * r : 16 * r + 16], ck_ref[r], dims, preferred_element_type=jnp.float32
        )
        parts.append(jnp.where(lanes < len_ref[r], score * SCORE_SCALE, MASKED_SCORE))
    score = jnp.concatenate(parts, axis=0)
    fresh_keys = jnp.concatenate([nk_ref[0], nk_ref[1]], axis=0)
    fresh_values = jnp.concatenate([nv_ref[0], nv_ref[1]], axis=0)
    fresh = lax.dot_general(query, fresh_keys, dims, preferred_element_type=jnp.float32) * SCORE_SCALE
    row, col = iota((QUERIES, 32), 0), iota((QUERIES, 32), 1)
    live = ((row >> 4) == (col & 15)) & ((col >> 4) <= ((row >> 3) & 1))
    fresh = jnp.where(live, fresh, MASKED_SCORE)
    peak = jnp.maximum(jnp.max(score, axis=1, keepdims=True), jnp.max(fresh, axis=1, keepdims=True))
    weight = jnp.exp2(score - peak)
    fresh_weight = jnp.exp2(fresh - peak)
    total = jnp.sum(weight, axis=1, keepdims=True) + jnp.sum(fresh_weight, axis=1, keepdims=True)
    m_ref[...] = jnp.broadcast_to(peak, (QUERIES, 128))
    l_ref[...] = jnp.broadcast_to(total, (QUERIES, 128))
    weight = weight.astype(jnp.bfloat16)
    acc = jnp.concatenate(
        [
            jnp.dot(weight[16 * r : 16 * r + 16], cv_ref[r], preferred_element_type=jnp.float32)
            for r in range(ROWS)
        ],
        axis=0,
    )
    acc_ref[...] = acc + jnp.dot(
        fresh_weight.astype(jnp.bfloat16), fresh_values, preferred_element_type=jnp.float32
    )


def resident(lengths, queries, cache_keys, cache_values, new_keys, new_values):
    wide = jax.ShapeDtypeStruct((QUERIES, 128), jnp.float32)
    return pl.pallas_call(
        resident_kernel,
        out_shape=(jax.ShapeDtypeStruct((QUERIES, 128), jnp.bfloat16), wide, wide, wide),
        in_specs=[SMEM] + [VMEM] * 5,
        out_specs=(VMEM,) * 4,
        scratch_shapes=[pltpu.VMEM((QUERIES, 128), jnp.float32)],
        compiler_params=PARAMS,
        cost_estimate=pl.CostEstimate(flops=20_000_000, bytes_accessed=1_500_000, transcendentals=40_000),
        name="resident",
    )(lengths, queries, cache_keys, cache_values, new_keys, new_values)


def merge_kernel(code_ref, recv_ref, q_ref, m_ref, l_ref, acc_ref, out_ref, turn_ref):
    wide = recv_ref[...].astype(jnp.float32).reshape(SLOTS, 2, 8, 128)
    even, odd = wide[:, 0], wide[:, 1]
    is_key = (iota((SLOTS, 8, 128), 1) & 1) == 0
    keys = jnp.where(is_key, even, pltpu.roll(odd, 1, 1)).reshape(SLOTS * 8, 128).astype(jnp.bfloat16)
    values = jnp.where(is_key, pltpu.roll(even, 7, 1), odd).reshape(SLOTS * 8, 128).astype(jnp.bfloat16)
    half = QUERIES // 2
    for request in range(2):
        rows = pl.ds(request * half, half)
        code = code_ref[...]
        length = jnp.where((code >> 4) == request, code & 15, 0)
        live = jnp.concatenate([length > t for t in range(8)], axis=1)
        score = lax.dot_general(
            q_ref[rows, :], keys, (((1,), (1,)), ((), ())), preferred_element_type=jnp.float32
        )
        score = jnp.where(live, score * SCORE_SCALE, MASKED_SCORE)
        old = m_ref[rows, :][:, 0:1]
        peak = jnp.maximum(jnp.max(score, axis=1, keepdims=True), old)
        weight = jnp.exp2(score - peak)
        keep = jnp.exp2(old - peak)
        total = jnp.sum(weight, axis=1, keepdims=True) + l_ref[rows, :][:, 0:1] * keep
        acc = jnp.dot(weight.astype(jnp.bfloat16), values, preferred_element_type=jnp.float32)
        turn_ref[rows, :] = (acc + acc_ref[rows, :] * keep) / total
    for step in range(2):
        for g in range(GROUP):
            out_ref[step, :, 128 * g : 128 * g + 128] = turn_ref[
                pl.ds(step * GROUP + g, ROWS, stride=2 * GROUP), :
            ].astype(jnp.bfloat16)


def merge(codes, received, query, peak, total, acc):
    return pl.pallas_call(
        merge_kernel,
        out_shape=jax.ShapeDtypeStruct((2, ROWS, GROUP * HEAD_DIM), jnp.bfloat16),
        in_specs=[VMEM] * 6,
        out_specs=VMEM,
        scratch_shapes=[pltpu.VMEM((QUERIES, 128), jnp.float32)],
        compiler_params=PARAMS,
        name="merge",
    )(codes, received, query, peak, total, acc)


def slot_codes(page_owner, page_request, page_length):
    own = lax.axis_index("pool")
    code = (page_length + 16 * page_request).reshape(POOL, PAGES)
    matched = page_owner.reshape(POOL, PAGES) == own
    position = iota((POOL, PAGES), 1)
    first = jnp.min(jnp.where(matched, position, PAGES), axis=1, keepdims=True)
    last = jnp.max(jnp.where(matched, position, -1), axis=1, keepdims=True)
    head = jnp.sum(jnp.where(position == first, code, 0), axis=1)
    tail = jnp.sum(jnp.where((position == last) & (last > first), code, 0), axis=1)
    slots = jnp.stack([head, tail], axis=1)
    return slots.reshape(16, 2, 2, 2).transpose(0, 2, 3, 1).reshape(1, SLOTS)


def body(
    queries,
    new_keys,
    new_values,
    cache_keys,
    cache_values,
    cache_lengths,
    handoff_kv,
    page_owner,
    page_request,
    page_length,
):
    pages = handoff_kv.reshape(PAGES, 2, KV_HEADS, 128).transpose(0, 2, 1, 3).reshape(PAGES * 16, 128)
    sent = pack(page_owner.reshape(24, 128), pages)
    arrived = lax.all_to_all(
        sent.reshape(TENSOR * POOL, 2 * CAP, 128), ("tensor", "pool"), split_axis=0, concat_axis=0, tiled=True
    )
    _, page_owner, page_request, page_length = lax.optimization_barrier(
        (sent, page_owner, page_request, page_length)
    )
    codes = slot_codes(page_owner, page_request, page_length)
    query, peak, total, acc = resident(cache_lengths, queries, cache_keys, cache_values, new_keys, new_values)
    return merge(codes, arrived.reshape(SLOTS * 16, 128), query, peak, total, acc)


def solution(mesh):
    return jax.shard_map(
        body,
        mesh=mesh,
        in_specs=(
            P(None, "pool", "tensor"),
            P(None, "pool", "tensor"),
            P(None, "pool", "tensor"),
            P("pool", None, "tensor"),
            P("pool", None, "tensor"),
            P("pool"),
            P("pool", None, "tensor", None, None),
            P(),
            P(),
            P(),
        ),
        out_specs=P(None, "pool", "tensor"),
        check_vma=False,
    )
```

```python
import jax
import jax.numpy as jnp
from jax import lax
from jax.experimental import pallas as pl
from jax.experimental.pallas import tpu as pltpu
from jax.sharding import PartitionSpec as P

HEADS = 64
KV_HEADS = 8
HEAD_DIM = 128
GROUP = HEADS // KV_HEADS
SAMPLES = 8
POOL = 64
TENSOR = 8
PAGES = 48
CAP = 2
ROWS = 16
RES_LEN = 128
SLOTS = POOL * CAP
QUERIES = 2 * ROWS * GROUP

MASKED_SCORE = -1e30
SCORE_SCALE = HEAD_DIM ** (-0.5) * 1.4426950408889634

VMEM = pl.BlockSpec(memory_space=pltpu.VMEM)
SMEM = pl.BlockSpec(memory_space=pltpu.SMEM)
HBM = pl.BlockSpec(memory_space=pltpu.HBM)
PARAMS = pltpu.CompilerParams(vmem_limit_bytes=32 * 1024 * 1024)


def iota(shape, axis):
    return lax.broadcasted_iota(jnp.int32, shape, axis)


def pack_kernel(owner_hbm, pages_hbm, out_hbm, owner_ref, pages_ref, wide_ref, out_ref, sems):
    fetch_pages = pltpu.make_async_copy(pages_hbm, pages_ref, sems.at[0])
    fetch_owners = pltpu.make_async_copy(owner_hbm, owner_ref, sems.at[1])
    fetch_owners.start()
    fetch_pages.start()
    start = lax.axis_index("pool") * PAGES
    row, lane = start // 128, lax.rem(start, 128)
    shift = lax.rem(128 - lane, 128)
    fetch_owners.wait()
    first = jnp.broadcast_to(owner_ref[pl.ds(row, 1), :], (8, 128))
    second = jnp.broadcast_to(owner_ref[pl.ds(jnp.minimum(row + 1, 23), 1), :], (8, 128))
    lanes = iota((8, 128), 1)
    owners = jnp.where(lanes < 128 - lane, pltpu.roll(first, shift, 1), pltpu.roll(second, shift, 1))
    across = jnp.broadcast_to(owners[0:1].astype(jnp.float32), (128, 128))
    down = across.T
    earlier = iota((128, 128), 0) < iota((128, 128), 1)
    rank = jnp.sum(jnp.where((across == down) & earlier, 1.0, 0.0), axis=0, keepdims=True)
    key = (owners * (2 * CAP)).astype(jnp.float32) + 2.0 * rank
    key = key.astype(jnp.int32)
    target = jnp.where(
        lanes < PAGES, key, jnp.where(lanes < 2 * PAGES, pltpu.roll(key, PAGES, 1) + 1, -1)
    )
    slots = jnp.where(iota((2 * SLOTS, 128), 0) == target[0:1], 1.0, 0.0).astype(jnp.bfloat16)
    fetch_pages.wait()
    wide_ref[...] = pages_ref[...].astype(jnp.float32)
    zeros = jnp.zeros((128 - 2 * PAGES, 128), jnp.bfloat16)
    stores = []
    for head in range(0, KV_HEADS, 2):
        block = jnp.concatenate(
            [
                jnp.concatenate(
                    [
                        wide_ref[pl.ds(2 * h + kv, PAGES, stride=2 * KV_HEADS), :].astype(jnp.bfloat16)
                        for kv in range(2)
                    ]
                    + [zeros],
                    axis=0,
                )
                for h in (head, head + 1)
            ],
            axis=1,
        )
        placed = jnp.dot(slots, block, preferred_element_type=jnp.float32).astype(jnp.bfloat16)
        out_ref[head * 256 : head * 256 + 256, :] = placed[:, 0:128]
        out_ref[head * 256 + 256 : head * 256 + 512, :] = placed[:, 128:256]
        rows = pl.ds(head * 256, 512)
        stores.append(pltpu.make_async_copy(out_ref.at[rows], out_hbm.at[rows], sems.at[2 + head // 2]))
        stores[-1].start()
    for store in stores:
        store.wait()


def pack(owners, pages):
    return pl.pallas_call(
        pack_kernel,
        out_shape=jax.ShapeDtypeStruct((KV_HEADS * SLOTS * 2, 128), jnp.bfloat16),
        in_specs=[HBM, HBM],
        out_specs=HBM,
        scratch_shapes=[
            pltpu.VMEM((24, 128), jnp.int32),
            pltpu.VMEM((PAGES * 2 * KV_HEADS, 128), jnp.bfloat16),
            pltpu.VMEM((PAGES * 2 * KV_HEADS, 128), jnp.float32),
            pltpu.VMEM((KV_HEADS * SLOTS * 2, 128), jnp.bfloat16),
            pltpu.SemaphoreType.DMA((6,)),
        ],
        name="pack",
    )(owners, pages)


def resident_kernel(len_ref, q_ref, ck_ref, cv_ref, nk_ref, nv_ref, qt_ref, m_ref, l_ref, acc_ref, turn_ref):
    for step in range(2):
        wide = q_ref[step].astype(jnp.float32)
        for g in range(GROUP):
            turn_ref[pl.ds(step * GROUP + g, ROWS, stride=2 * GROUP), :] = wide[:, 128 * g : 128 * g + 128]
    query = turn_ref[...].astype(jnp.bfloat16)
    qt_ref[...] = query
    dims = (((1,), (1,)), ((), ()))
    lanes = iota((16, 128), 1)
    parts = []
    for r in range(ROWS):
        score = lax.dot_general(
            query[16 * r : 16 * r + 16], ck_ref[r], dims, preferred_element_type=jnp.float32
        )
        parts.append(jnp.where(lanes < len_ref[r], score * SCORE_SCALE, MASKED_SCORE))
    score = jnp.concatenate(parts, axis=0)
    fresh_keys = jnp.concatenate([nk_ref[0], nk_ref[1]], axis=0)
    fresh_values = jnp.concatenate([nv_ref[0], nv_ref[1]], axis=0)
    fresh = lax.dot_general(query, fresh_keys, dims, preferred_element_type=jnp.float32) * SCORE_SCALE
    row, col = iota((QUERIES, 32), 0), iota((QUERIES, 32), 1)
    live = ((row >> 4) == (col & 15)) & ((col >> 4) <= ((row >> 3) & 1))
    fresh = jnp.where(live, fresh, MASKED_SCORE)
    peak = jnp.maximum(jnp.max(score, axis=1, keepdims=True), jnp.max(fresh, axis=1, keepdims=True))
    weight = jnp.exp2(score - peak)
    fresh_weight = jnp.exp2(fresh - peak)
    total = jnp.sum(weight, axis=1, keepdims=True) + jnp.sum(fresh_weight, axis=1, keepdims=True)
    m_ref[...] = jnp.broadcast_to(peak, (QUERIES, 128))
    l_ref[...] = jnp.broadcast_to(total, (QUERIES, 128))
    weight = weight.astype(jnp.bfloat16)
    acc = jnp.concatenate(
        [
            jnp.dot(weight[16 * r : 16 * r + 16], cv_ref[r], preferred_element_type=jnp.float32)
            for r in range(ROWS)
        ],
        axis=0,
    )
    acc_ref[...] = acc + jnp.dot(
        fresh_weight.astype(jnp.bfloat16), fresh_values, preferred_element_type=jnp.float32
    )


def resident(lengths, queries, cache_keys, cache_values, new_keys, new_values):
    wide = jax.ShapeDtypeStruct((QUERIES, 128), jnp.float32)
    return pl.pallas_call(
        resident_kernel,
        out_shape=(jax.ShapeDtypeStruct((QUERIES, 128), jnp.bfloat16), wide, wide, wide),
        in_specs=[SMEM] + [VMEM] * 5,
        out_specs=(VMEM,) * 4,
        scratch_shapes=[pltpu.VMEM((QUERIES, 128), jnp.float32)],
        compiler_params=PARAMS,
        cost_estimate=pl.CostEstimate(flops=20_000_000, bytes_accessed=1_500_000, transcendentals=40_000),
        name="resident",
    )(lengths, queries, cache_keys, cache_values, new_keys, new_values)


def merge_kernel(code_ref, recv_ref, q_ref, m_ref, l_ref, acc_ref, out_ref, turn_ref):
    wide = recv_ref[...].astype(jnp.float32).reshape(SLOTS, 2, 8, 128)
    even, odd = wide[:, 0], wide[:, 1]
    is_key = (iota((SLOTS, 8, 128), 1) & 1) == 0
    keys = jnp.where(is_key, even, pltpu.roll(odd, 1, 1)).reshape(SLOTS * 8, 128).astype(jnp.bfloat16)
    values = jnp.where(is_key, pltpu.roll(even, 7, 1), odd).reshape(SLOTS * 8, 128).astype(jnp.bfloat16)
    code = code_ref[...]
    bias = []
    for request in range(2):
        length = jnp.where((code >> 4) == request, code & 15, 0)
        bias.append(jnp.concatenate([jnp.where(length > t, 0.0, MASKED_SCORE) for t in range(8)], axis=1))
    half = QUERIES // 2
    score = lax.dot_general(
        q_ref[...], keys, (((1,), (1,)), ((), ())), preferred_element_type=jnp.float32
    )
    score = jnp.concatenate([score[:half] * SCORE_SCALE + bias[0], score[half:] * SCORE_SCALE + bias[1]], axis=0)
    old = m_ref[...][:, 0:1]
    peak = jnp.maximum(jnp.max(score, axis=1, keepdims=True), old)
    weight = jnp.exp2(score - peak)
    keep = jnp.exp2(old - peak)
    total = jnp.sum(weight, axis=1, keepdims=True) + l_ref[...][:, 0:1] * keep
    acc = jnp.dot(weight.astype(jnp.bfloat16), values, preferred_element_type=jnp.float32)
    turn_ref[...] = (acc + acc_ref[...] * keep) / total
    for step in range(2):
        for g in range(GROUP):
            out_ref[step, :, 128 * g : 128 * g + 128] = turn_ref[
                pl.ds(step * GROUP + g, ROWS, stride=2 * GROUP), :
            ].astype(jnp.bfloat16)


def merge(codes, received, query, peak, total, acc):
    return pl.pallas_call(
        merge_kernel,
        out_shape=jax.ShapeDtypeStruct((2, ROWS, GROUP * HEAD_DIM), jnp.bfloat16),
        in_specs=[VMEM] * 6,
        out_specs=VMEM,
        scratch_shapes=[pltpu.VMEM((QUERIES, 128), jnp.float32)],
        compiler_params=PARAMS,
        name="merge",
    )(codes, received, query, peak, total, acc)


def slot_codes(page_owner, page_request, page_length):
    own = lax.axis_index("pool")
    code = (page_length + 16 * page_request).reshape(POOL, PAGES)
    matched = page_owner.reshape(POOL, PAGES) == own
    position = iota((POOL, PAGES), 1)
    first = jnp.min(jnp.where(matched, position, PAGES), axis=1, keepdims=True)
    last = jnp.max(jnp.where(matched, position, -1), axis=1, keepdims=True)
    head = jnp.sum(jnp.where(position == first, code, 0), axis=1)
    tail = jnp.sum(jnp.where((position == last) & (last > first), code, 0), axis=1)
    slots = jnp.stack([head, tail], axis=1)
    return slots.reshape(16, 2, 2, 2).transpose(0, 2, 3, 1).reshape(1, SLOTS)


def body(
    queries,
    new_keys,
    new_values,
    cache_keys,
    cache_values,
    cache_lengths,
    handoff_kv,
    page_owner,
    page_request,
    page_length,
):
    pages = handoff_kv.reshape(PAGES, 2, KV_HEADS, 128).transpose(0, 2, 1, 3).reshape(PAGES * 16, 128)
    sent = pack(page_owner.reshape(24, 128), pages)
    arrived = lax.all_to_all(
        sent.reshape(TENSOR * POOL, 2 * CAP, 128), ("tensor", "pool"), split_axis=0, concat_axis=0, tiled=True
    )
    _, page_owner, page_request, page_length = lax.optimization_barrier(
        (sent, page_owner, page_request, page_length)
    )
    codes = slot_codes(page_owner, page_request, page_length)
    query, peak, total, acc = resident(cache_lengths, queries, cache_keys, cache_values, new_keys, new_values)
    return merge(codes, arrived.reshape(SLOTS * 16, 128), query, peak, total, acc)


def solution(mesh):
    return jax.shard_map(
        body,
        mesh=mesh,
        in_specs=(
            P(None, "pool", "tensor"),
            P(None, "pool", "tensor"),
            P(None, "pool", "tensor"),
            P("pool", None, "tensor"),
            P("pool", None, "tensor"),
            P("pool"),
            P("pool", None, "tensor", None, None),
            P(),
            P(),
            P(),
        ),
        out_specs=P(None, "pool", "tensor"),
        check_vma=False,
    )
```

```python
import jax
import jax.numpy as jnp
from jax import lax
from jax.experimental import pallas as pl
from jax.experimental.pallas import tpu as pltpu
from jax.sharding import PartitionSpec as P

HEADS = 64
KV_HEADS = 8
HEAD_DIM = 128
GROUP = HEADS // KV_HEADS
SAMPLES = 8
POOL = 64
TENSOR = 8
PAGES = 48
CAP = 2
ROWS = 16
RES_LEN = 128
SLOTS = POOL * CAP
QUERIES = 2 * ROWS * GROUP

MASKED_SCORE = -1e30
SCORE_SCALE = HEAD_DIM ** (-0.5) * 1.4426950408889634

POOL_ORDER = [(y * 8 + z) * 2 + core for core in range(2) for z in range(8) for y in range(4)]
HEAD_ORDER = [half * 4 + x for x in range(4) for half in range(2)]
EXCHANGE = [[p * TENSOR + t for p in POOL_ORDER for t in HEAD_ORDER]]

VMEM = pl.BlockSpec(memory_space=pltpu.VMEM)
SMEM = pl.BlockSpec(memory_space=pltpu.SMEM)
HBM = pl.BlockSpec(memory_space=pltpu.HBM)
PARAMS = pltpu.CompilerParams(vmem_limit_bytes=32 * 1024 * 1024)


def iota(shape, axis):
    return lax.broadcasted_iota(jnp.int32, shape, axis)


def pack_kernel(owner_hbm, pages_hbm, out_hbm, owner_ref, pages_ref, wide_ref, out_ref, sems):
    fetch_pages = pltpu.make_async_copy(pages_hbm, pages_ref, sems.at[0])
    fetch_owners = pltpu.make_async_copy(owner_hbm, owner_ref, sems.at[1])
    fetch_owners.start()
    fetch_pages.start()
    start = lax.axis_index("pool") * PAGES
    row, lane = start // 128, lax.rem(start, 128)
    shift = lax.rem(128 - lane, 128)
    fetch_owners.wait()
    first = jnp.broadcast_to(owner_ref[pl.ds(row, 1), :], (8, 128))
    second = jnp.broadcast_to(owner_ref[pl.ds(jnp.minimum(row + 1, 23), 1), :], (8, 128))
    lanes = iota((8, 128), 1)
    owners = jnp.where(lanes < 128 - lane, pltpu.roll(first, shift, 1), pltpu.roll(second, shift, 1))
    across = jnp.broadcast_to(owners[0:1].astype(jnp.float32), (128, 128))
    down = across.T
    earlier = iota((128, 128), 0) < iota((128, 128), 1)
    rank = jnp.sum(jnp.where((across == down) & earlier, 1.0, 0.0), axis=0, keepdims=True)
    place = (owners & 1) * 32 + ((owners >> 1) & 7) * 4 + (owners >> 4)
    key = (place * (2 * CAP)).astype(jnp.float32) + 2.0 * rank
    key = key.astype(jnp.int32)
    target = jnp.where(
        lanes < PAGES, key, jnp.where(lanes < 2 * PAGES, pltpu.roll(key, PAGES, 1) + 1, -1)
    )
    slots = jnp.where(iota((2 * SLOTS, 128), 0) == target[0:1], 1.0, 0.0).astype(jnp.bfloat16)
    fetch_pages.wait()
    wide_ref[...] = pages_ref[...].astype(jnp.float32)
    zeros = jnp.zeros((128 - 2 * PAGES, 128), jnp.bfloat16)
    first_half = iota((POOL // 2, 8, 128), 1) < 4
    stores = []
    for part in range(2):
        low, high = [], []
        for pair in range(2):
            heads = HEAD_ORDER[4 * part + 2 * pair : 4 * part + 2 * pair + 2]
            block = jnp.concatenate(
                [
                    jnp.concatenate(
                        [
                            wide_ref[pl.ds(2 * h + kv, PAGES, stride=2 * KV_HEADS), :].astype(jnp.bfloat16)
                            for kv in range(2)
                        ]
                        + [zeros],
                        axis=0,
                    )
                    for h in heads
                ],
                axis=1,
            )
            placed = jnp.dot(slots, block, preferred_element_type=jnp.float32)
            left = placed[:, 0:128].reshape(POOL // 2, 8, 128)
            right = placed[:, 128:256].reshape(POOL // 2, 8, 128)
            low.append(jnp.where(first_half, left, pltpu.roll(right, 4, 1)))
            high.append(jnp.where(first_half, pltpu.roll(left, 4, 1), right))
        rows = pl.ds(16 * part, 16)
        out_ref[:, 0, rows, :] = jnp.concatenate(low, axis=1).astype(jnp.bfloat16)
        out_ref[:, 1, rows, :] = jnp.concatenate(high, axis=1).astype(jnp.bfloat16)
        stores.append(
            pltpu.make_async_copy(out_ref.at[:, :, rows], out_hbm.at[:, :, rows], sems.at[2 + part])
        )
        stores[-1].start()
    for store in stores:
        store.wait()


def pack(owners, pages):
    return pl.pallas_call(
        pack_kernel,
        out_shape=jax.ShapeDtypeStruct((POOL // 2, 2, 4 * KV_HEADS, 128), jnp.bfloat16),
        in_specs=[HBM, HBM],
        out_specs=HBM,
        scratch_shapes=[
            pltpu.VMEM((24, 128), jnp.int32),
            pltpu.VMEM((PAGES * 2 * KV_HEADS, 128), jnp.bfloat16),
            pltpu.VMEM((PAGES * 2 * KV_HEADS, 128), jnp.float32),
            pltpu.VMEM((POOL // 2, 2, 4 * KV_HEADS, 128), jnp.bfloat16),
            pltpu.SemaphoreType.DMA((4,)),
        ],
        name="pack",
    )(owners, pages)


def resident_kernel(len_ref, q_ref, ck_ref, cv_ref, nk_ref, nv_ref, qt_ref, m_ref, l_ref, acc_ref, turn_ref):
    for step in range(2):
        wide = q_ref[step].astype(jnp.float32)
        for g in range(GROUP):
            turn_ref[pl.ds(step * GROUP + g, ROWS, stride=2 * GROUP), :] = wide[:, 128 * g : 128 * g + 128]
            block = pl.ds((step * GROUP + g) * ROWS, ROWS)
            qt_ref[block, :] = q_ref[step, :, 128 * g : 128 * g + 128]
    query = turn_ref[...].astype(jnp.bfloat16)
    dims = (((1,), (1,)), ((), ()))
    lanes = iota((16, 128), 1)
    parts = []
    for r in range(ROWS):
        score = lax.dot_general(
            query[16 * r : 16 * r + 16], ck_ref[r], dims, preferred_element_type=jnp.float32
        )
        parts.append(jnp.where(lanes < len_ref[r], score * SCORE_SCALE, MASKED_SCORE))
    score = jnp.concatenate(parts, axis=0)
    fresh_keys = jnp.concatenate([nk_ref[0], nk_ref[1]], axis=0)
    fresh_values = jnp.concatenate([nv_ref[0], nv_ref[1]], axis=0)
    fresh = lax.dot_general(query, fresh_keys, dims, preferred_element_type=jnp.float32) * SCORE_SCALE
    row, col = iota((QUERIES, 32), 0), iota((QUERIES, 32), 1)
    live = ((row >> 4) == (col & 15)) & ((col >> 4) <= ((row >> 3) & 1))
    fresh = jnp.where(live, fresh, MASKED_SCORE)
    peak = jnp.maximum(jnp.max(score, axis=1, keepdims=True), jnp.max(fresh, axis=1, keepdims=True))
    weight = jnp.exp2(score - peak)
    fresh_weight = jnp.exp2(fresh - peak)
    total = jnp.sum(weight, axis=1, keepdims=True) + jnp.sum(fresh_weight, axis=1, keepdims=True)
    weight = weight.astype(jnp.bfloat16)
    acc = jnp.concatenate(
        [
            jnp.dot(weight[16 * r : 16 * r + 16], cv_ref[r], preferred_element_type=jnp.float32)
            for r in range(ROWS)
        ],
        axis=0,
    )
    acc = acc + jnp.dot(fresh_weight.astype(jnp.bfloat16), fresh_values, preferred_element_type=jnp.float32)
    for result, result_ref in ((peak, m_ref), (total, l_ref), (acc, acc_ref)):
        turn_ref[...] = jnp.broadcast_to(result, (QUERIES, 128))
        for j in range(2 * GROUP):
            result_ref[ROWS * j : ROWS * j + ROWS, :] = turn_ref[pl.ds(j, ROWS, stride=2 * GROUP), :]


def resident(lengths, queries, cache_keys, cache_values, new_keys, new_values):
    wide = jax.ShapeDtypeStruct((QUERIES, 128), jnp.float32)
    return pl.pallas_call(
        resident_kernel,
        out_shape=(jax.ShapeDtypeStruct((QUERIES, 128), jnp.bfloat16), wide, wide, wide),
        in_specs=[SMEM] + [VMEM] * 5,
        out_specs=(VMEM,) * 4,
        scratch_shapes=[pltpu.VMEM((QUERIES, 128), jnp.float32)],
        compiler_params=PARAMS,
        cost_estimate=pl.CostEstimate(flops=20_000_000, bytes_accessed=1_500_000, transcendentals=40_000),
        name="resident",
    )(lengths, queries, cache_keys, cache_values, new_keys, new_values)


def merge_kernel(bias_ref, recv_ref, q_ref, m_ref, l_ref, acc_ref, out_ref):
    wide = recv_ref[...].astype(jnp.float32).reshape(SLOTS, 2, 8, 128)
    even, odd = wide[:, 0], wide[:, 1]
    is_key = (iota((SLOTS, 8, 128), 1) & 1) == 0
    keys = jnp.where(is_key, even, pltpu.roll(odd, 1, 1)).reshape(SLOTS * 8, 128).astype(jnp.bfloat16)
    values = jnp.where(is_key, pltpu.roll(even, 7, 1), odd).reshape(SLOTS * 8, 128).astype(jnp.bfloat16)
    score = lax.dot_general(
        q_ref[...], keys, (((1,), (1,)), ((), ())), preferred_element_type=jnp.float32
    )
    bias = bias_ref[...].reshape(1, 2, 1, SLOTS * 8)
    score = (score.reshape(2 * GROUP, 2, SAMPLES, SLOTS * 8) * SCORE_SCALE + bias).reshape(QUERIES, SLOTS * 8)
    old = m_ref[...][:, 0:1]
    peak = jnp.maximum(jnp.max(score, axis=1, keepdims=True), old)
    weight = jnp.exp2(score - peak)
    keep = jnp.exp2(old - peak)
    total = jnp.sum(weight, axis=1, keepdims=True) + l_ref[...][:, 0:1] * keep
    acc = jnp.dot(weight.astype(jnp.bfloat16), values, preferred_element_type=jnp.float32)
    pieces = ((acc + acc_ref[...] * keep) / total).astype(jnp.bfloat16)
    for step in range(2):
        for g in range(GROUP):
            at = (step * GROUP + g) * ROWS
            out_ref[step, :, 128 * g : 128 * g + 128] = pieces[at : at + ROWS]


def merge(bias, received, query, peak, total, acc):
    return pl.pallas_call(
        merge_kernel,
        out_shape=jax.ShapeDtypeStruct((2, ROWS, GROUP * HEAD_DIM), jnp.bfloat16),
        in_specs=[VMEM] * 6,
        out_specs=VMEM,
        compiler_params=PARAMS,
        name="merge",
    )(bias, received, query, peak, total, acc)


def received_bias(page_owner, page_request, page_length):
    own = lax.axis_index("pool")
    code = (page_length + 16 * page_request).reshape(POOL, PAGES)
    matched = page_owner.reshape(POOL, PAGES) == own
    position = iota((POOL, PAGES), 1)
    first = jnp.min(jnp.where(matched, position, PAGES), axis=1, keepdims=True)
    last = jnp.max(jnp.where(matched, position, -1), axis=1, keepdims=True)
    head = jnp.sum(jnp.where(position == first, code, 0), axis=1)
    tail = jnp.sum(jnp.where((position == last) & (last > first), code, 0), axis=1)
    slots = jnp.stack([head, tail], axis=1).reshape(4, 8, 2, CAP).transpose(2, 1, 0, 3)
    shape = (2, POOL, 2, 2, CAP, 2)
    slots = jnp.broadcast_to(slots.reshape(1, POOL, 1, 1, CAP, 1), shape)
    token = 4 * iota(shape, 3) + 2 * iota(shape, 2) + iota(shape, 5)
    live = ((slots >> 4) == iota(shape, 0)) & ((slots & 15) > token)
    return jnp.where(live, 0.0, MASKED_SCORE).reshape(2, SLOTS * 8)


def body(
    queries,
    new_keys,
    new_values,
    cache_keys,
    cache_values,
    cache_lengths,
    handoff_kv,
    page_owner,
    page_request,
    page_length,
):
    pages = handoff_kv.reshape(PAGES, 2, KV_HEADS, 128).transpose(0, 2, 1, 3).reshape(PAGES * 16, 128)
    sent = pack(page_owner.reshape(24, 128), pages)
    arrived = lax.all_to_all(
        sent.reshape(TENSOR * POOL, 2 * CAP, 128),
        ("pool", "tensor"),
        split_axis=0,
        concat_axis=0,
        axis_index_groups=EXCHANGE,
        tiled=True,
    )
    _, page_owner, page_request, page_length = lax.optimization_barrier(
        (sent, page_owner, page_request, page_length)
    )
    bias = received_bias(page_owner, page_request, page_length)
    query, peak, total, acc = resident(cache_lengths, queries, cache_keys, cache_values, new_keys, new_values)
    return merge(bias, arrived.reshape(SLOTS * 16, 128), query, peak, total, acc)


def solution(mesh):
    return jax.shard_map(
        body,
        mesh=mesh,
        in_specs=(
            P(None, "pool", "tensor"),
            P(None, "pool", "tensor"),
            P(None, "pool", "tensor"),
            P("pool", None, "tensor"),
            P("pool", None, "tensor"),
            P("pool"),
            P("pool", None, "tensor", None, None),
            P(),
            P(),
            P(),
        ),
        out_specs=P(None, "pool", "tensor"),
        check_vma=False,
    )
```

```python
import jax
import jax.numpy as jnp
from jax import lax
from jax.experimental import pallas as pl
from jax.experimental.pallas import tpu as pltpu
from jax.sharding import PartitionSpec as P

HEADS = 64
KV_HEADS = 8
HEAD_DIM = 128
GROUP = HEADS // KV_HEADS
SAMPLES = 8
POOL = 64
TENSOR = 8
PAGES = 48
CAP = 2
ROWS = 16
RES_LEN = 128
SLOTS = POOL * CAP
QUERIES = 2 * ROWS * GROUP

MASKED_SCORE = -1e30
SCORE_SCALE = HEAD_DIM ** (-0.5) * 1.4426950408889634

POOL_ORDER = [(y * 8 + z) * 2 + core for core in range(2) for z in range(8) for y in range(4)]
HEAD_ORDER = [half * 4 + x for x in range(4) for half in range(2)]
EXCHANGE = [[p * TENSOR + t for p in POOL_ORDER for t in HEAD_ORDER]]

VMEM = pl.BlockSpec(memory_space=pltpu.VMEM)
SMEM = pl.BlockSpec(memory_space=pltpu.SMEM)
HBM = pl.BlockSpec(memory_space=pltpu.HBM)
PARAMS = pltpu.CompilerParams(vmem_limit_bytes=32 * 1024 * 1024)


def iota(shape, axis):
    return lax.broadcasted_iota(jnp.int32, shape, axis)


def pack_kernel(owner_hbm, pages_hbm, out_hbm, owner_ref, pages_ref, wide_ref, out_ref, sems):
    fetch_pages = pltpu.make_async_copy(pages_hbm, pages_ref, sems.at[0])
    fetch_owners = pltpu.make_async_copy(owner_hbm, owner_ref, sems.at[1])
    fetch_owners.start()
    fetch_pages.start()
    start = lax.axis_index("pool") * PAGES
    row, lane = start // 128, lax.rem(start, 128)
    shift = lax.rem(128 - lane, 128)
    fetch_owners.wait()
    first = jnp.broadcast_to(owner_ref[pl.ds(row, 1), :], (8, 128))
    second = jnp.broadcast_to(owner_ref[pl.ds(jnp.minimum(row + 1, 23), 1), :], (8, 128))
    lanes = iota((8, 128), 1)
    owners = jnp.where(lanes < 128 - lane, pltpu.roll(first, shift, 1), pltpu.roll(second, shift, 1))
    across = jnp.broadcast_to(owners[0:1].astype(jnp.float32), (128, 128))
    down = across.T
    earlier = iota((128, 128), 0) < iota((128, 128), 1)
    rank = jnp.sum(jnp.where((across == down) & earlier, 1.0, 0.0), axis=0, keepdims=True)
    place = (owners & 1) * 32 + ((owners >> 1) & 7) * 4 + (owners >> 4)
    key = (place * (2 * CAP)).astype(jnp.float32) + 2.0 * rank
    key = key.astype(jnp.int32)
    target = jnp.where(
        lanes < PAGES, key, jnp.where(lanes < 2 * PAGES, pltpu.roll(key, PAGES, 1) + 1, -1)
    )
    slots = jnp.where(iota((2 * SLOTS, 128), 0) == target[0:1], 1.0, 0.0).astype(jnp.bfloat16)
    fetch_pages.wait()
    wide_ref[...] = pages_ref[...].astype(jnp.float32)
    zeros = jnp.zeros((128 - 2 * PAGES, 128), jnp.bfloat16)
    first_half = iota((POOL // 2, 8, 128), 1) < 4
    stores = []
    for part in range(2):
        low, high = [], []
        for pair in range(2):
            heads = HEAD_ORDER[4 * part + 2 * pair : 4 * part + 2 * pair + 2]
            block = jnp.concatenate(
                [
                    jnp.concatenate(
                        [
                            wide_ref[pl.ds(2 * h + kv, PAGES, stride=2 * KV_HEADS), :].astype(jnp.bfloat16)
                            for kv in range(2)
                        ]
                        + [zeros],
                        axis=0,
                    )
                    for h in heads
                ],
                axis=1,
            )
            placed = jnp.dot(slots, block, preferred_element_type=jnp.float32)
            left = placed[:, 0:128].reshape(POOL // 2, 8, 128)
            right = placed[:, 128:256].reshape(POOL // 2, 8, 128)
            low.append(jnp.where(first_half, left, pltpu.roll(right, 4, 1)))
            high.append(jnp.where(first_half, pltpu.roll(left, 4, 1), right))
        rows = pl.ds(16 * part, 16)
        out_ref[:, 0, rows, :] = jnp.concatenate(low, axis=1).astype(jnp.bfloat16)
        out_ref[:, 1, rows, :] = jnp.concatenate(high, axis=1).astype(jnp.bfloat16)
        stores.append(
            pltpu.make_async_copy(out_ref.at[:, :, rows], out_hbm.at[:, :, rows], sems.at[2 + part])
        )
        stores[-1].start()
    for store in stores:
        store.wait()


def pack(owners, pages):
    return pl.pallas_call(
        pack_kernel,
        out_shape=jax.ShapeDtypeStruct((POOL // 2, 2, 4 * KV_HEADS, 128), jnp.bfloat16),
        in_specs=[HBM, HBM],
        out_specs=HBM,
        scratch_shapes=[
            pltpu.VMEM((24, 128), jnp.int32),
            pltpu.VMEM((PAGES * 2 * KV_HEADS, 128), jnp.bfloat16),
            pltpu.VMEM((PAGES * 2 * KV_HEADS, 128), jnp.float32),
            pltpu.VMEM((POOL // 2, 2, 4 * KV_HEADS, 128), jnp.bfloat16),
            pltpu.SemaphoreType.DMA((4,)),
        ],
        name="pack",
    )(owners, pages)


def resident_kernel(len_ref, q_ref, ck_ref, nk_ref, nv_ref, qt_ref, score_ref, m_ref, fresh_ref, turn_ref):
    for step in range(2):
        wide = q_ref[step].astype(jnp.float32)
        for g in range(GROUP):
            turn_ref[pl.ds(step * GROUP + g, ROWS, stride=2 * GROUP), :] = wide[:, 128 * g : 128 * g + 128]
    query = turn_ref[...].astype(jnp.bfloat16)
    qt_ref[...] = query
    dims = (((1,), (1,)), ((), ()))
    lanes = iota((16, 128), 1)
    parts = []
    for r in range(ROWS):
        score = lax.dot_general(
            query[16 * r : 16 * r + 16], ck_ref[r], dims, preferred_element_type=jnp.float32
        )
        parts.append(jnp.where(lanes < len_ref[r], score * SCORE_SCALE, MASKED_SCORE))
    score = jnp.concatenate(parts, axis=0)
    rest = jnp.zeros((128 - 2 * ROWS, 128), jnp.bfloat16)
    fresh_keys = jnp.concatenate([nk_ref[0], nk_ref[1], rest], axis=0)
    fresh_ref[...] = jnp.concatenate([nv_ref[0], nv_ref[1], rest], axis=0)
    fresh = lax.dot_general(query, fresh_keys, dims, preferred_element_type=jnp.float32) * SCORE_SCALE
    row, col = iota((QUERIES, 128), 0), iota((QUERIES, 128), 1)
    live = ((row >> 4) == (col & 15)) & ((col >> 4) <= ((row >> 3) & 1))
    fresh = jnp.where(live, fresh, MASKED_SCORE)
    score_ref[:, 0:128] = score
    score_ref[:, 128:256] = fresh
    peak = jnp.max(jnp.maximum(score, fresh), axis=1, keepdims=True)
    m_ref[...] = jnp.broadcast_to(peak, (QUERIES, 128))


def resident(lengths, queries, cache_keys, new_keys, new_values):
    return pl.pallas_call(
        resident_kernel,
        out_shape=(
            jax.ShapeDtypeStruct((QUERIES, 128), jnp.bfloat16),
            jax.ShapeDtypeStruct((QUERIES, 256), jnp.float32),
            jax.ShapeDtypeStruct((QUERIES, 128), jnp.float32),
            jax.ShapeDtypeStruct((128, 128), jnp.bfloat16),
        ),
        in_specs=[SMEM] + [VMEM] * 4,
        out_specs=(VMEM,) * 4,
        scratch_shapes=[pltpu.VMEM((QUERIES, 128), jnp.float32)],
        compiler_params=PARAMS,
        cost_estimate=pl.CostEstimate(flops=10_000_000, bytes_accessed=1_000_000, transcendentals=0),
        name="resident",
    )(lengths, queries, cache_keys, new_keys, new_values)


def merge_kernel(bias_ref, recv_ref, q_ref, score_ref, m_ref, cv_ref, fresh_ref, out_ref, turn_ref):
    wide = recv_ref[...].astype(jnp.float32).reshape(SLOTS, 2, 8, 128)
    even, odd = wide[:, 0], wide[:, 1]
    is_key = (iota((SLOTS, 8, 128), 1) & 1) == 0
    keys = jnp.where(is_key, even, pltpu.roll(odd, 1, 1)).reshape(SLOTS * 8, 128).astype(jnp.bfloat16)
    values = jnp.where(is_key, pltpu.roll(even, 7, 1), odd).reshape(SLOTS * 8, 128).astype(jnp.bfloat16)
    score = lax.dot_general(
        q_ref[...], keys, (((1,), (1,)), ((), ())), preferred_element_type=jnp.float32
    )
    half = QUERIES // 2
    score = jnp.concatenate(
        [score[:half] * SCORE_SCALE + bias_ref[0:1, :], score[half:] * SCORE_SCALE + bias_ref[1:2, :]], axis=0
    )
    peak = jnp.maximum(jnp.max(score, axis=1, keepdims=True), m_ref[...][:, 0:1])
    weight = jnp.exp2(score - peak)
    own = jnp.exp2(score_ref[...] - peak)
    total = jnp.sum(weight, axis=1, keepdims=True) + jnp.sum(own, axis=1, keepdims=True)
    own = own.astype(jnp.bfloat16)
    held = jnp.concatenate(
        [
            jnp.dot(own[16 * r : 16 * r + 16, 0:128], cv_ref[r], preferred_element_type=jnp.float32)
            for r in range(ROWS)
        ],
        axis=0,
    )
    acc = jnp.dot(
        jnp.concatenate([weight.astype(jnp.bfloat16), own[:, 128:256]], axis=1),
        jnp.concatenate([values, fresh_ref[...]], axis=0),
        preferred_element_type=jnp.float32,
    )
    turn_ref[...] = (acc + held) / total
    for step in range(2):
        for g in range(GROUP):
            out_ref[step, :, 128 * g : 128 * g + 128] = turn_ref[
                pl.ds(step * GROUP + g, ROWS, stride=2 * GROUP), :
            ].astype(jnp.bfloat16)


def merge(bias, received, query, score, peak, cache_values, fresh_values):
    return pl.pallas_call(
        merge_kernel,
        out_shape=jax.ShapeDtypeStruct((2, ROWS, GROUP * HEAD_DIM), jnp.bfloat16),
        in_specs=[VMEM] * 7,
        out_specs=VMEM,
        scratch_shapes=[pltpu.VMEM((QUERIES, 128), jnp.float32)],
        compiler_params=PARAMS,
        name="merge",
    )(bias, received, query, score, peak, cache_values, fresh_values)


def received_bias(page_owner, page_request, page_length):
    own = lax.axis_index("pool")
    code = (page_length + 16 * page_request).reshape(POOL, PAGES)
    matched = page_owner.reshape(POOL, PAGES) == own
    position = iota((POOL, PAGES), 1)
    first = jnp.min(jnp.where(matched, position, PAGES), axis=1, keepdims=True)
    last = jnp.max(jnp.where(matched, position, -1), axis=1, keepdims=True)
    head = jnp.sum(jnp.where(position == first, code, 0), axis=1)
    tail = jnp.sum(jnp.where((position == last) & (last > first), code, 0), axis=1)
    slots = jnp.stack([head, tail], axis=1).reshape(4, 8, 2, CAP).transpose(2, 1, 0, 3)
    shape = (2, POOL, 2, 2, CAP, 2)
    slots = jnp.broadcast_to(slots.reshape(1, POOL, 1, 1, CAP, 1), shape)
    token = 4 * iota(shape, 3) + 2 * iota(shape, 2) + iota(shape, 5)
    live = ((slots >> 4) == iota(shape, 0)) & ((slots & 15) > token)
    return jnp.where(live, 0.0, MASKED_SCORE).reshape(2, SLOTS * 8)


def body(
    queries,
    new_keys,
    new_values,
    cache_keys,
    cache_values,
    cache_lengths,
    handoff_kv,
    page_owner,
    page_request,
    page_length,
):
    pages = handoff_kv.reshape(PAGES, 2, KV_HEADS, 128).transpose(0, 2, 1, 3).reshape(PAGES * 16, 128)
    sent = pack(page_owner.reshape(24, 128), pages)
    arrived = lax.all_to_all(
        sent.reshape(TENSOR * POOL, 2 * CAP, 128),
        ("pool", "tensor"),
        split_axis=0,
        concat_axis=0,
        axis_index_groups=EXCHANGE,
        tiled=True,
    )
    _, page_owner, page_request, page_length = lax.optimization_barrier(
        (sent, page_owner, page_request, page_length)
    )
    bias = received_bias(page_owner, page_request, page_length)
    query, score, peak, fresh_values = resident(cache_lengths, queries, cache_keys, new_keys, new_values)
    return merge(bias, arrived.reshape(SLOTS * 16, 128), query, score, peak, cache_values, fresh_values)


def solution(mesh):
    return jax.shard_map(
        body,
        mesh=mesh,
        in_specs=(
            P(None, "pool", "tensor"),
            P(None, "pool", "tensor"),
            P(None, "pool", "tensor"),
            P("pool", None, "tensor"),
            P("pool", None, "tensor"),
            P("pool"),
            P("pool", None, "tensor", None, None),
            P(),
            P(),
            P(),
        ),
        out_specs=P(None, "pool", "tensor"),
        check_vma=False,
    )
```

```python
import functools

import jax
import jax.numpy as jnp
from jax import lax
from jax.experimental import pallas as pl
from jax.experimental.pallas import tpu as pltpu
from jax.sharding import PartitionSpec as P

HEADS = 64
KV_HEADS = 8
HEAD_DIM = 128
GROUP = HEADS // KV_HEADS
SAMPLES = 8
POOL = 64
TENSOR = 8
PAGES = 48
CAP = 2
ROWS = 16
RES_LEN = 128
SLOTS = POOL * CAP
QUERIES = 2 * ROWS * GROUP

MASKED_SCORE = -1e30
SCORE_SCALE = HEAD_DIM ** (-0.5) * 1.4426950408889634

POOL_ORDER = [(y * 8 + z) * 2 + core for core in range(2) for z in range(8) for y in range(4)]
HEAD_ORDER = [half * 4 + x for x in range(4) for half in range(2)]
EXCHANGE = [[p * TENSOR + t for p in POOL_ORDER for t in HEAD_ORDER]]

VMEM = pl.BlockSpec(memory_space=pltpu.VMEM)
SMEM = pl.BlockSpec(memory_space=pltpu.SMEM)
HBM = pl.BlockSpec(memory_space=pltpu.HBM)
PARAMS = pltpu.CompilerParams(vmem_limit_bytes=32 * 1024 * 1024)


def iota(shape, axis):
    return lax.broadcasted_iota(jnp.int32, shape, axis)


def pack_kernel(owner_hbm, pages_hbm, out_hbm, owner_ref, pages_ref, wide_ref, out_ref, sems):
    fetch_pages = pltpu.make_async_copy(pages_hbm, pages_ref, sems.at[0])
    fetch_owners = pltpu.make_async_copy(owner_hbm, owner_ref, sems.at[1])
    fetch_owners.start()
    fetch_pages.start()
    start = lax.axis_index("pool") * PAGES
    row, lane = start // 128, lax.rem(start, 128)
    shift = lax.rem(128 - lane, 128)
    fetch_owners.wait()
    first = jnp.broadcast_to(owner_ref[pl.ds(row, 1), :], (8, 128))
    second = jnp.broadcast_to(owner_ref[pl.ds(jnp.minimum(row + 1, 23), 1), :], (8, 128))
    lanes = iota((8, 128), 1)
    owners = jnp.where(lanes < 128 - lane, pltpu.roll(first, shift, 1), pltpu.roll(second, shift, 1))
    across = jnp.broadcast_to(owners[0:1].astype(jnp.float32), (128, 128))
    down = across.T
    earlier = iota((128, 128), 0) < iota((128, 128), 1)
    rank = jnp.sum(jnp.where((across == down) & earlier, 1.0, 0.0), axis=0, keepdims=True)
    place = (owners & 1) * 32 + ((owners >> 1) & 7) * 4 + (owners >> 4)
    key = (place * (2 * CAP)).astype(jnp.float32) + 2.0 * rank
    key = key.astype(jnp.int32)
    target = jnp.where(
        lanes < PAGES, key, jnp.where(lanes < 2 * PAGES, pltpu.roll(key, PAGES, 1) + 1, -1)
    )
    slots = jnp.where(iota((2 * SLOTS, 128), 0) == target[0:1], 1.0, 0.0).astype(jnp.bfloat16)
    fetch_pages.wait()
    wide_ref[...] = pages_ref[...].astype(jnp.float32)
    zeros = jnp.zeros((128 - 2 * PAGES, 128), jnp.bfloat16)
    first_half = iota((POOL // 2, 8, 128), 1) < 4
    stores = []
    for part in range(2):
        low, high = [], []
        for pair in range(2):
            heads = HEAD_ORDER[4 * part + 2 * pair : 4 * part + 2 * pair + 2]
            block = jnp.concatenate(
                [
                    jnp.concatenate(
                        [
                            wide_ref[pl.ds(2 * h + kv, PAGES, stride=2 * KV_HEADS), :].astype(jnp.bfloat16)
                            for kv in range(2)
                        ]
                        + [zeros],
                        axis=0,
                    )
                    for h in heads
                ],
                axis=1,
            )
            placed = jnp.dot(slots, block, preferred_element_type=jnp.float32)
            left = placed[:, 0:128].reshape(POOL // 2, 8, 128)
            right = placed[:, 128:256].reshape(POOL // 2, 8, 128)
            low.append(jnp.where(first_half, left, pltpu.roll(right, 4, 1)))
            high.append(jnp.where(first_half, pltpu.roll(left, 4, 1), right))
        rows = pl.ds(16 * part, 16)
        out_ref[:, 0, rows, :] = jnp.concatenate(low, axis=1).astype(jnp.bfloat16)
        out_ref[:, 1, rows, :] = jnp.concatenate(high, axis=1).astype(jnp.bfloat16)
        stores.append(
            pltpu.make_async_copy(out_ref.at[:, :, rows], out_hbm.at[:, :, rows], sems.at[2 + part])
        )
        stores[-1].start()
    for store in stores:
        store.wait()


def pack(owners, pages):
    return pl.pallas_call(
        pack_kernel,
        out_shape=jax.ShapeDtypeStruct((POOL // 2, 2, 4 * KV_HEADS, 128), jnp.bfloat16),
        in_specs=[HBM, HBM],
        out_specs=HBM,
        scratch_shapes=[
            pltpu.VMEM((24, 128), jnp.int32),
            pltpu.VMEM((PAGES * 2 * KV_HEADS, 128), jnp.bfloat16),
            pltpu.VMEM((PAGES * 2 * KV_HEADS, 128), jnp.float32),
            pltpu.VMEM((POOL // 2, 2, 4 * KV_HEADS, 128), jnp.bfloat16),
            pltpu.SemaphoreType.DMA((4,)),
        ],
        name="pack",
    )(owners, pages)


def resident_kernel(len_ref, q_ref, ck_ref, nk_ref, nv_ref, qt_ref, score_ref, m_ref, fresh_ref, turn_ref):
    for step in range(2):
        wide = q_ref[step].astype(jnp.float32)
        for g in range(GROUP):
            turn_ref[pl.ds(step * GROUP + g, ROWS, stride=2 * GROUP), :] = wide[:, 128 * g : 128 * g + 128]
    query = turn_ref[...].astype(jnp.bfloat16)
    qt_ref[...] = query
    dims = (((1,), (1,)), ((), ()))
    lanes = iota((16, 128), 1)
    parts = []
    for r in range(ROWS):
        score = lax.dot_general(
            query[16 * r : 16 * r + 16], ck_ref[r], dims, preferred_element_type=jnp.float32
        )
        parts.append(jnp.where(lanes < len_ref[r], score * SCORE_SCALE, MASKED_SCORE))
    score = jnp.concatenate(parts, axis=0)
    rest = jnp.zeros((128 - 2 * ROWS, 128), jnp.bfloat16)
    fresh_keys = jnp.concatenate([nk_ref[0], nk_ref[1], rest], axis=0)
    fresh_ref[...] = jnp.concatenate([nv_ref[0], nv_ref[1], rest], axis=0)
    fresh = lax.dot_general(query, fresh_keys, dims, preferred_element_type=jnp.float32) * SCORE_SCALE
    row, col = iota((QUERIES, 128), 0), iota((QUERIES, 128), 1)
    live = ((row >> 4) == (col & 15)) & ((col >> 4) <= ((row >> 3) & 1))
    fresh = jnp.where(live, fresh, MASKED_SCORE)
    score_ref[:, 0:128] = score
    score_ref[:, 128:256] = fresh
    peak = jnp.max(jnp.maximum(score, fresh), axis=1, keepdims=True)
    m_ref[...] = jnp.broadcast_to(peak, (QUERIES, 128))


def resident(lengths, queries, cache_keys, new_keys, new_values):
    return pl.pallas_call(
        resident_kernel,
        out_shape=(
            jax.ShapeDtypeStruct((QUERIES, 128), jnp.bfloat16),
            jax.ShapeDtypeStruct((QUERIES, 256), jnp.float32),
            jax.ShapeDtypeStruct((QUERIES, 128), jnp.float32),
            jax.ShapeDtypeStruct((128, 128), jnp.bfloat16),
        ),
        in_specs=[SMEM] + [VMEM] * 4,
        out_specs=(VMEM,) * 4,
        scratch_shapes=[pltpu.VMEM((QUERIES, 128), jnp.float32)],
        compiler_params=PARAMS,
        cost_estimate=pl.CostEstimate(flops=10_000_000, bytes_accessed=1_000_000, transcendentals=0),
        name="resident",
    )(lengths, queries, cache_keys, new_keys, new_values)


def merge_kernel(bias_ref, recv_ref, q_ref, score_ref, m_ref, cv_ref, fresh_ref, out_ref, turn_ref):
    wide = recv_ref[...].astype(jnp.float32).reshape(SLOTS, 2, 8, 128)
    even, odd = wide[:, 0], wide[:, 1]
    is_key = (iota((SLOTS, 8, 128), 1) & 1) == 0
    keys = jnp.where(is_key, even, pltpu.roll(odd, 1, 1)).reshape(SLOTS * 8, 128).astype(jnp.bfloat16)
    values = jnp.where(is_key, pltpu.roll(even, 7, 1), odd).reshape(SLOTS * 8, 128).astype(jnp.bfloat16)
    score = lax.dot_general(
        q_ref[...], keys, (((1,), (1,)), ((), ())), preferred_element_type=jnp.float32
    )
    half = QUERIES // 2
    score = jnp.concatenate(
        [score[:half] * SCORE_SCALE + bias_ref[0:1, :], score[half:] * SCORE_SCALE + bias_ref[1:2, :]], axis=0
    )
    tiles = [score[:, 128 * t : 128 * t + 128] for t in range(8)]
    peak = functools.reduce(jnp.maximum, tiles, m_ref[...])
    peak = jnp.max(peak, axis=1, keepdims=True)
    tiles = [jnp.exp2(tile - peak) for tile in tiles + [score_ref[:, 0:128], score_ref[:, 128:256]]]
    total = jnp.sum(functools.reduce(jnp.add, tiles), axis=1, keepdims=True)
    tiles = [tile.astype(jnp.bfloat16) for tile in tiles]
    held = []
    for r in range(0, ROWS, 2):
        both = jnp.dot(
            tiles[8][16 * r : 16 * r + 32],
            jnp.concatenate([cv_ref[r], cv_ref[r + 1]], axis=1),
            preferred_element_type=jnp.float32,
        )
        held += [both[0:16, 0:128], both[16:32, 128:256]]
    held = jnp.concatenate(held, axis=0)
    acc = jnp.dot(
        jnp.concatenate(tiles[:8] + tiles[9:], axis=1),
        jnp.concatenate([values, fresh_ref[...]], axis=0),
        preferred_element_type=jnp.float32,
    )
    turn_ref[...] = (acc + held) / total
    for step in range(2):
        for g in range(GROUP):
            out_ref[step, :, 128 * g : 128 * g + 128] = turn_ref[
                pl.ds(step * GROUP + g, ROWS, stride=2 * GROUP), :
            ].astype(jnp.bfloat16)


def merge(bias, received, query, score, peak, cache_values, fresh_values):
    return pl.pallas_call(
        merge_kernel,
        out_shape=jax.ShapeDtypeStruct((2, ROWS, GROUP * HEAD_DIM), jnp.bfloat16),
        in_specs=[VMEM] * 7,
        out_specs=VMEM,
        scratch_shapes=[pltpu.VMEM((QUERIES, 128), jnp.float32)],
        compiler_params=PARAMS,
        name="merge",
    )(bias, received, query, score, peak, cache_values, fresh_values)


def received_bias(page_owner, page_request, page_length):
    own = lax.axis_index("pool")
    code = (page_length + 16 * page_request).reshape(POOL, PAGES)
    matched = page_owner.reshape(POOL, PAGES) == own
    position = iota((POOL, PAGES), 1)
    first = jnp.min(jnp.where(matched, position, PAGES), axis=1, keepdims=True)
    last = jnp.max(jnp.where(matched, position, -1), axis=1, keepdims=True)
    head = jnp.sum(jnp.where(position == first, code, 0), axis=1)
    tail = jnp.sum(jnp.where((position == last) & (last > first), code, 0), axis=1)
    slots = jnp.stack([head, tail], axis=1).reshape(4, 8, 2, CAP).transpose(2, 1, 0, 3)
    shape = (2, POOL, 2, 2, CAP, 2)
    slots = jnp.broadcast_to(slots.reshape(1, POOL, 1, 1, CAP, 1), shape)
    token = 4 * iota(shape, 3) + 2 * iota(shape, 2) + iota(shape, 5)
    live = ((slots >> 4) == iota(shape, 0)) & ((slots & 15) > token)
    return jnp.where(live, 0.0, MASKED_SCORE).reshape(2, SLOTS * 8)


def body(
    queries,
    new_keys,
    new_values,
    cache_keys,
    cache_values,
    cache_lengths,
    handoff_kv,
    page_owner,
    page_request,
    page_length,
):
    pages = handoff_kv.reshape(PAGES, 2, KV_HEADS, 128).transpose(0, 2, 1, 3).reshape(PAGES * 16, 128)
    sent = pack(page_owner.reshape(24, 128), pages)
    arrived = lax.all_to_all(
        sent.reshape(TENSOR * POOL, 2 * CAP, 128),
        ("pool", "tensor"),
        split_axis=0,
        concat_axis=0,
        axis_index_groups=EXCHANGE,
        tiled=True,
    )
    _, page_owner, page_request, page_length = lax.optimization_barrier(
        (sent, page_owner, page_request, page_length)
    )
    bias = received_bias(page_owner, page_request, page_length)
    query, score, peak, fresh_values = resident(cache_lengths, queries, cache_keys, new_keys, new_values)
    return merge(bias, arrived.reshape(SLOTS * 16, 128), query, score, peak, cache_values, fresh_values)


def solution(mesh):
    return jax.shard_map(
        body,
        mesh=mesh,
        in_specs=(
            P(None, "pool", "tensor"),
            P(None, "pool", "tensor"),
            P(None, "pool", "tensor"),
            P("pool", None, "tensor"),
            P("pool", None, "tensor"),
            P("pool"),
            P("pool", None, "tensor", None, None),
            P(),
            P(),
            P(),
        ),
        out_specs=P(None, "pool", "tensor"),
        check_vma=False,
    )
```

```python
import functools

import jax
import jax.numpy as jnp
from jax import lax
from jax.experimental import pallas as pl
from jax.experimental.pallas import tpu as pltpu
from jax.sharding import PartitionSpec as P

HEADS = 64
KV_HEADS = 8
HEAD_DIM = 128
GROUP = HEADS // KV_HEADS
SAMPLES = 8
POOL = 64
TENSOR = 8
PAGES = 48
CAP = 2
ROWS = 16
RES_LEN = 128
SLOTS = POOL * CAP
QUERIES = 2 * ROWS * GROUP

MASKED_SCORE = -1e30
SCORE_SCALE = HEAD_DIM ** (-0.5) * 1.4426950408889634

POOL_ORDER = [(y * 8 + z) * 2 + core for core in range(2) for z in range(8) for y in range(4)]
HEAD_ORDER = [half * 4 + x for x in range(4) for half in range(2)]
EXCHANGE = [[p * TENSOR + t for p in POOL_ORDER for t in HEAD_ORDER]]

VMEM = pl.BlockSpec(memory_space=pltpu.VMEM)
SMEM = pl.BlockSpec(memory_space=pltpu.SMEM)
HBM = pl.BlockSpec(memory_space=pltpu.HBM)
PARAMS = pltpu.CompilerParams(vmem_limit_bytes=32 * 1024 * 1024)


def iota(shape, axis):
    return lax.broadcasted_iota(jnp.int32, shape, axis)


def pack_kernel(owner_hbm, pages_hbm, out_hbm, owner_ref, pages_ref, wide_ref, out_ref, sems):
    half = PAGES * KV_HEADS
    fetch_pages = [
        pltpu.make_async_copy(
            pages_hbm.at[pl.ds(half * i, half)], pages_ref.at[pl.ds(half * i, half)], sems.at[3 * i]
        )
        for i in range(2)
    ]
    fetch_owners = pltpu.make_async_copy(owner_hbm, owner_ref, sems.at[1])
    fetch_owners.start()
    fetch_pages[0].start()
    fetch_pages[1].start(priority=1)
    start = lax.axis_index("pool") * PAGES
    row, lane = start // 128, lax.rem(start, 128)
    shift = lax.rem(128 - lane, 128)
    fetch_owners.wait()
    first = jnp.broadcast_to(owner_ref[pl.ds(row, 1), :], (8, 128))
    second = jnp.broadcast_to(owner_ref[pl.ds(jnp.minimum(row + 1, 23), 1), :], (8, 128))
    lanes = iota((8, 128), 1)
    owners = jnp.where(lanes < 128 - lane, pltpu.roll(first, shift, 1), pltpu.roll(second, shift, 1))
    across = jnp.broadcast_to(owners[0:1].astype(jnp.float32), (128, 128))
    down = across.T
    earlier = iota((128, 128), 0) < iota((128, 128), 1)
    rank = jnp.sum(jnp.where((across == down) & earlier, 1.0, 0.0), axis=0, keepdims=True)
    place = (owners & 1) * 32 + ((owners >> 1) & 7) * 4 + (owners >> 4)
    key = (place * (2 * CAP)).astype(jnp.float32) + 2.0 * rank
    key = key.astype(jnp.int32)
    target = jnp.where(
        lanes < PAGES, key, jnp.where(lanes < 2 * PAGES, pltpu.roll(key, PAGES, 1) + 1, -1)
    )
    slots = jnp.where(iota((2 * SLOTS, 128), 0) == target[0:1], 1.0, 0.0).astype(jnp.bfloat16)
    for i in range(2):
        fetch_pages[i].wait()
        wide_ref[pl.ds(half * i, half), :] = pages_ref[pl.ds(half * i, half), :].astype(jnp.float32)
    zeros = jnp.zeros((128 - 2 * PAGES, 128), jnp.bfloat16)
    first_half = iota((POOL // 2, 8, 128), 1) < 4
    stores = []
    for part in range(2):
        low, high = [], []
        for pair in range(2):
            heads = HEAD_ORDER[4 * part + 2 * pair : 4 * part + 2 * pair + 2]
            block = jnp.concatenate(
                [
                    jnp.concatenate(
                        [
                            wide_ref[pl.ds(2 * h + kv, PAGES, stride=2 * KV_HEADS), :].astype(jnp.bfloat16)
                            for kv in range(2)
                        ]
                        + [zeros],
                        axis=0,
                    )
                    for h in heads
                ],
                axis=1,
            )
            placed = jnp.dot(slots, block, preferred_element_type=jnp.float32)
            left = placed[:, 0:128].reshape(POOL // 2, 8, 128)
            right = placed[:, 128:256].reshape(POOL // 2, 8, 128)
            low.append(jnp.where(first_half, left, pltpu.roll(right, 4, 1)))
            high.append(jnp.where(first_half, pltpu.roll(left, 4, 1), right))
        rows = pl.ds(16 * part, 16)
        out_ref[:, 0, rows, :] = jnp.concatenate(low, axis=1).astype(jnp.bfloat16)
        out_ref[:, 1, rows, :] = jnp.concatenate(high, axis=1).astype(jnp.bfloat16)
        stores.append(
            pltpu.make_async_copy(out_ref.at[:, :, rows], out_hbm.at[:, :, rows], sems.at[4 + part])
        )
        stores[-1].start()
    for store in stores:
        store.wait()


def pack(owners, pages):
    return pl.pallas_call(
        pack_kernel,
        out_shape=jax.ShapeDtypeStruct((POOL // 2, 2, 4 * KV_HEADS, 128), jnp.bfloat16),
        in_specs=[HBM, HBM],
        out_specs=HBM,
        scratch_shapes=[
            pltpu.VMEM((24, 128), jnp.int32),
            pltpu.VMEM((PAGES * 2 * KV_HEADS, 128), jnp.bfloat16),
            pltpu.VMEM((PAGES * 2 * KV_HEADS, 128), jnp.float32),
            pltpu.VMEM((POOL // 2, 2, 4 * KV_HEADS, 128), jnp.bfloat16),
            pltpu.SemaphoreType.DMA((6,)),
        ],
        name="pack",
    )(owners, pages)


def resident_kernel(len_ref, q_ref, ck_ref, nk_ref, nv_ref, qt_ref, score_ref, m_ref, fresh_ref, turn_ref):
    for step in range(2):
        wide = q_ref[step].astype(jnp.float32)
        for g in range(GROUP):
            turn_ref[pl.ds(step * GROUP + g, ROWS, stride=2 * GROUP), :] = wide[:, 128 * g : 128 * g + 128]
    query = turn_ref[...].astype(jnp.bfloat16)
    qt_ref[...] = query
    dims = (((1,), (1,)), ((), ()))
    lanes = iota((16, 128), 1)
    parts = []
    for r in range(ROWS):
        score = lax.dot_general(
            query[16 * r : 16 * r + 16], ck_ref[r], dims, preferred_element_type=jnp.float32
        )
        parts.append(jnp.where(lanes < len_ref[r], score * SCORE_SCALE, MASKED_SCORE))
    score = jnp.concatenate(parts, axis=0)
    rest = jnp.zeros((128 - 2 * ROWS, 128), jnp.bfloat16)
    fresh_keys = jnp.concatenate([nk_ref[0], nk_ref[1], rest], axis=0)
    fresh_ref[...] = jnp.concatenate([nv_ref[0], nv_ref[1], rest], axis=0)
    fresh = lax.dot_general(query, fresh_keys, dims, preferred_element_type=jnp.float32) * SCORE_SCALE
    row, col = iota((QUERIES, 128), 0), iota((QUERIES, 128), 1)
    live = ((row >> 4) == (col & 15)) & ((col >> 4) <= ((row >> 3) & 1))
    fresh = jnp.where(live, fresh, MASKED_SCORE)
    score_ref[:, 0:128] = score
    score_ref[:, 128:256] = fresh
    peak = jnp.max(jnp.maximum(score, fresh), axis=1, keepdims=True)
    m_ref[...] = jnp.broadcast_to(peak, (QUERIES, 128))


def resident(lengths, queries, cache_keys, new_keys, new_values):
    return pl.pallas_call(
        resident_kernel,
        out_shape=(
            jax.ShapeDtypeStruct((QUERIES, 128), jnp.bfloat16),
            jax.ShapeDtypeStruct((QUERIES, 256), jnp.float32),
            jax.ShapeDtypeStruct((QUERIES, 128), jnp.float32),
            jax.ShapeDtypeStruct((128, 128), jnp.bfloat16),
        ),
        in_specs=[SMEM] + [VMEM] * 4,
        out_specs=(VMEM,) * 4,
        scratch_shapes=[pltpu.VMEM((QUERIES, 128), jnp.float32)],
        compiler_params=PARAMS,
        cost_estimate=pl.CostEstimate(flops=10_000_000, bytes_accessed=1_000_000, transcendentals=0),
        name="resident",
    )(lengths, queries, cache_keys, new_keys, new_values)


def merge_kernel(bias_ref, recv_ref, q_ref, score_ref, m_ref, cv_ref, fresh_ref, out_ref, turn_ref):
    wide = recv_ref[...].astype(jnp.float32).reshape(SLOTS, 2, 8, 128)
    even, odd = wide[:, 0], wide[:, 1]
    is_key = (iota((SLOTS, 8, 128), 1) & 1) == 0
    keys = jnp.where(is_key, even, pltpu.roll(odd, 1, 1)).reshape(SLOTS * 8, 128).astype(jnp.bfloat16)
    values = jnp.where(is_key, pltpu.roll(even, 7, 1), odd).reshape(SLOTS * 8, 128).astype(jnp.bfloat16)
    score = lax.dot_general(
        q_ref[...], keys, (((1,), (1,)), ((), ())), preferred_element_type=jnp.float32
    )
    half = QUERIES // 2
    score = jnp.concatenate(
        [score[:half] * SCORE_SCALE + bias_ref[0:1, :], score[half:] * SCORE_SCALE + bias_ref[1:2, :]], axis=0
    )
    tiles = [score[:, 128 * t : 128 * t + 128] for t in range(8)]
    peak = functools.reduce(jnp.maximum, tiles, m_ref[...])
    peak = jnp.max(peak, axis=1, keepdims=True)
    tiles = [jnp.exp2(tile - peak) for tile in tiles + [score_ref[:, 0:128], score_ref[:, 128:256]]]
    total = jnp.sum(functools.reduce(jnp.add, tiles), axis=1, keepdims=True)
    tiles = [tile.astype(jnp.bfloat16) for tile in tiles]
    held = []
    for r in range(0, ROWS, 2):
        both = jnp.dot(
            tiles[8][16 * r : 16 * r + 32],
            jnp.concatenate([cv_ref[r], cv_ref[r + 1]], axis=1),
            preferred_element_type=jnp.float32,
        )
        held += [both[0:16, 0:128], both[16:32, 128:256]]
    held = jnp.concatenate(held, axis=0)
    acc = jnp.dot(
        jnp.concatenate(tiles[:8] + tiles[9:], axis=1),
        jnp.concatenate([values, fresh_ref[...]], axis=0),
        preferred_element_type=jnp.float32,
    )
    turn_ref[...] = (acc + held) / total
    for step in range(2):
        for g in range(GROUP):
            out_ref[step, :, 128 * g : 128 * g + 128] = turn_ref[
                pl.ds(step * GROUP + g, ROWS, stride=2 * GROUP), :
            ].astype(jnp.bfloat16)


def merge(bias, received, query, score, peak, cache_values, fresh_values):
    return pl.pallas_call(
        merge_kernel,
        out_shape=jax.ShapeDtypeStruct((2, ROWS, GROUP * HEAD_DIM), jnp.bfloat16),
        in_specs=[VMEM] * 7,
        out_specs=VMEM,
        scratch_shapes=[pltpu.VMEM((QUERIES, 128), jnp.float32)],
        compiler_params=PARAMS,
        name="merge",
    )(bias, received, query, score, peak, cache_values, fresh_values)


def received_bias(page_owner, page_request, page_length):
    own = lax.axis_index("pool")
    code = (page_length + 16 * page_request).reshape(POOL, PAGES)
    matched = page_owner.reshape(POOL, PAGES) == own
    position = iota((POOL, PAGES), 1)
    first = jnp.min(jnp.where(matched, position, PAGES), axis=1, keepdims=True)
    last = jnp.max(jnp.where(matched, position, -1), axis=1, keepdims=True)
    head = jnp.sum(jnp.where(position == first, code, 0), axis=1)
    tail = jnp.sum(jnp.where((position == last) & (last > first), code, 0), axis=1)
    slots = jnp.stack([head, tail], axis=1).reshape(4, 8, 2, CAP).transpose(2, 1, 0, 3)
    shape = (2, POOL, 2, 2, CAP, 2)
    slots = jnp.broadcast_to(slots.reshape(1, POOL, 1, 1, CAP, 1), shape)
    token = 4 * iota(shape, 3) + 2 * iota(shape, 2) + iota(shape, 5)
    live = ((slots >> 4) == iota(shape, 0)) & ((slots & 15) > token)
    return jnp.where(live, 0.0, MASKED_SCORE).reshape(2, SLOTS * 8)


def body(
    queries,
    new_keys,
    new_values,
    cache_keys,
    cache_values,
    cache_lengths,
    handoff_kv,
    page_owner,
    page_request,
    page_length,
):
    pages = handoff_kv.reshape(PAGES, 2, KV_HEADS, 128).transpose(0, 2, 1, 3).reshape(PAGES * 16, 128)
    sent = pack(page_owner.reshape(24, 128), pages)
    arrived = lax.all_to_all(
        sent.reshape(TENSOR * POOL, 2 * CAP, 128),
        ("pool", "tensor"),
        split_axis=0,
        concat_axis=0,
        axis_index_groups=EXCHANGE,
        tiled=True,
    )
    _, page_owner, page_request, page_length = lax.optimization_barrier(
        (sent, page_owner, page_request, page_length)
    )
    bias = received_bias(page_owner, page_request, page_length)
    query, score, peak, fresh_values = resident(cache_lengths, queries, cache_keys, new_keys, new_values)
    return merge(bias, arrived.reshape(SLOTS * 16, 128), query, score, peak, cache_values, fresh_values)


def solution(mesh):
    return jax.shard_map(
        body,
        mesh=mesh,
        in_specs=(
            P(None, "pool", "tensor"),
            P(None, "pool", "tensor"),
            P(None, "pool", "tensor"),
            P("pool", None, "tensor"),
            P("pool", None, "tensor"),
            P("pool"),
            P("pool", None, "tensor", None, None),
            P(),
            P(),
            P(),
        ),
        out_specs=P(None, "pool", "tensor"),
        check_vma=False,
    )
```

```python
import functools

import jax
import jax.numpy as jnp
from jax import lax
from jax.experimental import pallas as pl
from jax.experimental.pallas import tpu as pltpu
from jax.sharding import PartitionSpec as P

HEADS = 64
KV_HEADS = 8
HEAD_DIM = 128
GROUP = HEADS // KV_HEADS
SAMPLES = 8
POOL = 64
TENSOR = 8
PAGES = 48
CAP = 2
ROWS = 16
RES_LEN = 128
SLOTS = POOL * CAP
QUERIES = 2 * ROWS * GROUP

MASKED_SCORE = -1e30
SCORE_SCALE = HEAD_DIM ** (-0.5) * 1.4426950408889634

POOL_ORDER = [(y * 8 + z) * 2 + core for core in range(2) for z in range(8) for y in range(4)]
HEAD_ORDER = [half * 4 + x for x in range(4) for half in range(2)]
EXCHANGE = [[p * TENSOR + t for p in POOL_ORDER for t in HEAD_ORDER]]

VMEM = pl.BlockSpec(memory_space=pltpu.VMEM)
SMEM = pl.BlockSpec(memory_space=pltpu.SMEM)
HBM = pl.BlockSpec(memory_space=pltpu.HBM)
PARAMS = pltpu.CompilerParams(vmem_limit_bytes=32 * 1024 * 1024)


def iota(shape, axis):
    return lax.broadcasted_iota(jnp.int32, shape, axis)


def pack_kernel(owner_hbm, pages_hbm, out_hbm, owner_ref, pages_ref, wide_ref, out_ref, sems):
    half = PAGES * KV_HEADS
    fetch_pages = [
        pltpu.make_async_copy(
            pages_hbm.at[pl.ds(half * i, half)], pages_ref.at[pl.ds(half * i, half)], sems.at[3 * i]
        )
        for i in range(2)
    ]
    fetch_owners = pltpu.make_async_copy(owner_hbm, owner_ref, sems.at[1])
    fetch_owners.start()
    fetch_pages[0].start()
    fetch_pages[1].start(priority=1)
    start = lax.axis_index("pool") * PAGES
    row, lane = start // 128, lax.rem(start, 128)
    shift = lax.rem(128 - lane, 128)
    fetch_owners.wait()
    first = jnp.broadcast_to(owner_ref[pl.ds(row, 1), :], (8, 128))
    second = jnp.broadcast_to(owner_ref[pl.ds(jnp.minimum(row + 1, 23), 1), :], (8, 128))
    lanes = iota((8, 128), 1)
    owners = jnp.where(lanes < 128 - lane, pltpu.roll(first, shift, 1), pltpu.roll(second, shift, 1))
    across = jnp.broadcast_to(owners[0:1].astype(jnp.float32), (128, 128))
    down = across.T
    earlier = iota((128, 128), 0) < iota((128, 128), 1)
    rank = jnp.sum(jnp.where((across == down) & earlier, 1.0, 0.0), axis=0, keepdims=True)
    place = (owners & 1) * 32 + ((owners >> 1) & 7) * 4 + (owners >> 4)
    key = (place * (2 * CAP)).astype(jnp.float32) + 2.0 * rank
    key = key.astype(jnp.int32)
    target = jnp.where(
        lanes < PAGES, key, jnp.where(lanes < 2 * PAGES, pltpu.roll(key, PAGES, 1) + 1, -1)
    )
    slots = jnp.where(iota((2 * SLOTS, 128), 0) == target[0:1], 1.0, 0.0).astype(jnp.bfloat16)
    for i in range(2):
        fetch_pages[i].wait()
        wide_ref[pl.ds(half * i, half), :] = pages_ref[pl.ds(half * i, half), :].astype(jnp.float32)
    zeros = jnp.zeros((128 - 2 * PAGES, 128), jnp.bfloat16)
    first_half = iota((POOL // 2, 8, 128), 1) < 4
    stores = []
    for part in range(2):
        low, high = [], []
        for pair in range(2):
            heads = HEAD_ORDER[4 * part + 2 * pair : 4 * part + 2 * pair + 2]
            block = jnp.concatenate(
                [
                    jnp.concatenate(
                        [
                            wide_ref[pl.ds(2 * h + kv, PAGES, stride=2 * KV_HEADS), :].astype(jnp.bfloat16)
                            for kv in range(2)
                        ]
                        + [zeros],
                        axis=0,
                    )
                    for h in heads
                ],
                axis=1,
            )
            placed = jnp.dot(slots, block, preferred_element_type=jnp.float32)
            left = placed[:, 0:128].reshape(POOL // 2, 8, 128)
            right = placed[:, 128:256].reshape(POOL // 2, 8, 128)
            low.append(jnp.where(first_half, left, pltpu.roll(right, 4, 1)))
            high.append(jnp.where(first_half, pltpu.roll(left, 4, 1), right))
        rows = pl.ds(16 * part, 16)
        out_ref[:, 0, rows, :] = jnp.concatenate(low, axis=1).astype(jnp.bfloat16)
        out_ref[:, 1, rows, :] = jnp.concatenate(high, axis=1).astype(jnp.bfloat16)
        stores.append(
            pltpu.make_async_copy(out_ref.at[:, :, rows], out_hbm.at[:, :, rows], sems.at[4 + part])
        )
        stores[-1].start()
    for store in stores:
        store.wait()


def pack(owners, pages):
    return pl.pallas_call(
        pack_kernel,
        out_shape=jax.ShapeDtypeStruct((POOL // 2, 2, 4 * KV_HEADS, 128), jnp.bfloat16),
        in_specs=[HBM, HBM],
        out_specs=HBM,
        scratch_shapes=[
            pltpu.VMEM((24, 128), jnp.int32),
            pltpu.VMEM((PAGES * 2 * KV_HEADS, 128), jnp.bfloat16),
            pltpu.VMEM((PAGES * 2 * KV_HEADS, 128), jnp.float32),
            pltpu.VMEM((POOL // 2, 2, 4 * KV_HEADS, 128), jnp.bfloat16),
            pltpu.SemaphoreType.DMA((6,)),
        ],
        name="pack",
    )(owners, pages)


def resident_kernel(len_ref, q_ref, ck_ref, nk_ref, nv_ref, qt_ref, score_ref, m_ref, fresh_ref, turn_ref):
    for step in range(2):
        wide = q_ref[step].astype(jnp.float32)
        for g in range(GROUP):
            turn_ref[pl.ds(step * GROUP + g, ROWS, stride=2 * GROUP), :] = wide[:, 128 * g : 128 * g + 128]
    query = turn_ref[...].astype(jnp.bfloat16)
    qt_ref[...] = query
    dims = (((1,), (1,)), ((), ()))
    lanes = iota((16, 128), 1)
    parts = []
    for r in range(ROWS):
        score = lax.dot_general(
            query[16 * r : 16 * r + 16], ck_ref[r], dims, preferred_element_type=jnp.float32
        )
        parts.append(jnp.where(lanes < len_ref[r], score * SCORE_SCALE, MASKED_SCORE))
    score = jnp.concatenate(parts, axis=0)
    rest = jnp.zeros((128 - 2 * ROWS, 128), jnp.bfloat16)
    fresh_keys = jnp.concatenate([nk_ref[0], nk_ref[1], rest], axis=0)
    fresh_ref[...] = jnp.concatenate([nv_ref[0], nv_ref[1], rest], axis=0)
    fresh = lax.dot_general(query, fresh_keys, dims, preferred_element_type=jnp.float32) * SCORE_SCALE
    row, col = iota((QUERIES, 128), 0), iota((QUERIES, 128), 1)
    live = ((row >> 4) == (col & 15)) & ((col >> 4) <= ((row >> 3) & 1))
    fresh = jnp.where(live, fresh, MASKED_SCORE)
    score_ref[:, 0:128] = score
    score_ref[:, 128:256] = fresh
    peak = jnp.max(jnp.maximum(score, fresh), axis=1, keepdims=True)
    m_ref[...] = jnp.broadcast_to(peak, (QUERIES, 128))


def resident(lengths, queries, cache_keys, new_keys, new_values):
    return pl.pallas_call(
        resident_kernel,
        out_shape=(
            jax.ShapeDtypeStruct((QUERIES, 128), jnp.bfloat16),
            jax.ShapeDtypeStruct((QUERIES, 256), jnp.float32),
            jax.ShapeDtypeStruct((QUERIES, 128), jnp.float32),
            jax.ShapeDtypeStruct((128, 128), jnp.bfloat16),
        ),
        in_specs=[SMEM] + [VMEM] * 4,
        out_specs=(VMEM,) * 4,
        scratch_shapes=[pltpu.VMEM((QUERIES, 128), jnp.float32)],
        compiler_params=PARAMS,
        cost_estimate=pl.CostEstimate(flops=10_000_000, bytes_accessed=1_000_000, transcendentals=0),
        name="resident",
    )(lengths, queries, cache_keys, new_keys, new_values)


def merge_kernel(bias_ref, recv_ref, q_ref, score_ref, m_ref, cv_ref, fresh_ref, out_ref, turn_ref):
    wide = recv_ref[...].astype(jnp.float32).reshape(SLOTS, 2, 8, 128)
    even, odd = wide[:, 0], wide[:, 1]
    is_key = (iota((SLOTS, 8, 128), 1) & 1) == 0
    keys = jnp.where(is_key, even, pltpu.roll(odd, 1, 1)).reshape(SLOTS * 8, 128).astype(jnp.bfloat16)
    values = jnp.where(is_key, pltpu.roll(even, 7, 1), odd).reshape(SLOTS * 8, 128).astype(jnp.bfloat16)
    score = lax.dot_general(
        q_ref[...], keys, (((1,), (1,)), ((), ())), preferred_element_type=jnp.float32
    )
    half = QUERIES // 2
    score = jnp.concatenate(
        [score[:half] * SCORE_SCALE + bias_ref[0:1, :], score[half:] * SCORE_SCALE + bias_ref[1:2, :]], axis=0
    )
    tiles = [score[:, 128 * t : 128 * t + 128] for t in range(8)]
    peak = functools.reduce(jnp.maximum, tiles, m_ref[...])
    peak = jnp.max(peak, axis=1, keepdims=True)
    tiles = [jnp.exp2(tile - peak) for tile in tiles + [score_ref[:, 0:128], score_ref[:, 128:256]]]
    total = jnp.sum(functools.reduce(jnp.add, tiles), axis=1, keepdims=True)
    tiles = [tile.astype(jnp.bfloat16) for tile in tiles]
    acc = jnp.dot(
        jnp.concatenate(tiles[:8] + tiles[9:], axis=1),
        jnp.concatenate([values, fresh_ref[...]], axis=0),
        preferred_element_type=jnp.float32,
    )
    held = []
    for r in range(0, ROWS, 2):
        both = jnp.dot(
            tiles[8][16 * r : 16 * r + 32],
            jnp.concatenate([cv_ref[r], cv_ref[r + 1]], axis=1),
            preferred_element_type=jnp.float32,
        )
        held += [both[0:16, 0:128], both[16:32, 128:256]]
    held = jnp.concatenate(held, axis=0)
    turn_ref[...] = (acc + held) / total
    for step in range(2):
        for g in range(GROUP):
            out_ref[step, :, 128 * g : 128 * g + 128] = turn_ref[
                pl.ds(step * GROUP + g, ROWS, stride=2 * GROUP), :
            ].astype(jnp.bfloat16)


def merge(bias, received, query, score, peak, cache_values, fresh_values):
    return pl.pallas_call(
        merge_kernel,
        out_shape=jax.ShapeDtypeStruct((2, ROWS, GROUP * HEAD_DIM), jnp.bfloat16),
        in_specs=[VMEM] * 7,
        out_specs=VMEM,
        scratch_shapes=[pltpu.VMEM((QUERIES, 128), jnp.float32)],
        compiler_params=PARAMS,
        name="merge",
    )(bias, received, query, score, peak, cache_values, fresh_values)


def received_bias(page_owner, page_request, page_length):
    own = lax.axis_index("pool")
    code = (page_length + 16 * page_request).reshape(POOL, PAGES)
    matched = page_owner.reshape(POOL, PAGES) == own
    position = iota((POOL, PAGES), 1)
    first = jnp.min(jnp.where(matched, position, PAGES), axis=1, keepdims=True)
    last = jnp.max(jnp.where(matched, position, -1), axis=1, keepdims=True)
    head = jnp.sum(jnp.where(position == first, code, 0), axis=1)
    tail = jnp.sum(jnp.where((position == last) & (last > first), code, 0), axis=1)
    slots = jnp.stack([head, tail], axis=1).reshape(4, 8, 2, CAP).transpose(2, 1, 0, 3)
    shape = (2, POOL, 2, 2, CAP, 2)
    slots = jnp.broadcast_to(slots.reshape(1, POOL, 1, 1, CAP, 1), shape)
    token = 4 * iota(shape, 3) + 2 * iota(shape, 2) + iota(shape, 5)
    live = ((slots >> 4) == iota(shape, 0)) & ((slots & 15) > token)
    return jnp.where(live, 0.0, MASKED_SCORE).reshape(2, SLOTS * 8)


def body(
    queries,
    new_keys,
    new_values,
    cache_keys,
    cache_values,
    cache_lengths,
    handoff_kv,
    page_owner,
    page_request,
    page_length,
):
    pages = handoff_kv.reshape(PAGES, 2, KV_HEADS, 128).transpose(0, 2, 1, 3).reshape(PAGES * 16, 128)
    sent = pack(page_owner.reshape(24, 128), pages)
    arrived = lax.all_to_all(
        sent.reshape(TENSOR * POOL, 2 * CAP, 128),
        ("pool", "tensor"),
        split_axis=0,
        concat_axis=0,
        axis_index_groups=EXCHANGE,
        tiled=True,
    )
    _, page_owner, page_request, page_length = lax.optimization_barrier(
        (sent, page_owner, page_request, page_length)
    )
    bias = received_bias(page_owner, page_request, page_length)
    query, score, peak, fresh_values = resident(cache_lengths, queries, cache_keys, new_keys, new_values)
    return merge(bias, arrived.reshape(SLOTS * 16, 128), query, score, peak, cache_values, fresh_values)


def solution(mesh):
    return jax.shard_map(
        body,
        mesh=mesh,
        in_specs=(
            P(None, "pool", "tensor"),
            P(None, "pool", "tensor"),
            P(None, "pool", "tensor"),
            P("pool", None, "tensor"),
            P("pool", None, "tensor"),
            P("pool"),
            P("pool", None, "tensor", None, None),
            P(),
            P(),
            P(),
        ),
        out_specs=P(None, "pool", "tensor"),
        check_vma=False,
    )
```
